128 devices in a mesh: tm: 4 (over x), mesh: 32 (over y, z, core).
Axes of the slice: x: 4, y: 4, z: 4, core: 2. Of those that a mesh axis runs over, the one named last changes fastest.
Arguments:
- right_sides: bfloat16 [8, 4096, 512], P('tm', 'mesh'), may hold values from -6 to 6
- diag_inverse: bfloat16 [8, 4096, 4096], P('tm', 'mesh'), may hold values from -0.09375 to 0.09375
- coupling: bfloat16 [8, 4096, 4096], P('tm', 'mesh'), may hold values from -0.0625 to 0.0625
- carry_in: bfloat16 [4096, 512], P('mesh'), may hold values from -6 to 6
- arrow_blocks: bfloat16 [8, 64, 4096], P('tm', None, 'mesh'), may hold values from -0.03125 to 0.03125
- tip_right: float32 [64, 512], replicated, may hold values from -6 to 6
- tip_inverse: float32 [64, 64], replicated, may hold values from -0.75 to 0.75
Outputs:
- forward_state: bfloat16 [8, 4096, 512], P('tm', 'mesh')
- tip_solution: float32 [64, 512], replicated
The draws below stay inside these ranges and needn't reach their ends.
All inputs are finite; a program needn't handle non-finite values.
Results may differ from the reference program's by a relative error of at most 0.011.
Values may be sent and summed in bfloat16 or wider, within the bound.
A program may use at most 64 MiB of HBM per device.

```python
import jax
import jax.numpy as jnp
from jax import lax

NB = 4096
FE = 64
R = 512
TIMES = 8


def steps_of(own_key, extent, split, least, high):
    def one(position, parts):
        steps = jax.random.uniform(jax.random.fold_in(jax.random.fold_in(own_key, 6), position), (parts,), jnp.float32, least / len(split), high / len(split))
        return jnp.repeat(jnp.exp(steps), extent[position] // parts).reshape((-1,) + (1,) * (len(extent) - position - 1))

    gain = one(*split[0])
    for cut in split[1:]:
        gain = gain * one(*cut)
    return gain


def normal_values(key, shape, scale, limit, cuts=(), dtype=jnp.bfloat16):
    factor_of = steps_of(key, shape, cuts, -0.22, 0.18) if cuts else 1.0
    result = jax.random.normal(key, shape, jnp.float32) * scale * factor_of
    return jnp.minimum(jnp.maximum(result, -limit), limit).astype(dtype)


def setup_inputs(seed: int = 0) -> dict:
    streams_of = jax.random.split(jax.random.key(seed), 8)
    right_sides = normal_values(streams_of[0], (TIMES, NB, R), 1.0, 6.0, ((0, 4), (1, 32)))
    diag_inverse = normal_values(streams_of[1], (TIMES, NB, NB), NB ** -0.5, 0.09375, ((0, 4), (1, 32)))
    coupling = normal_values(streams_of[2], (TIMES, NB, NB), (2 * NB) ** -0.5, 0.0625, ((0, 4), (1, 32)))
    carry_in = normal_values(streams_of[3], (NB, R), 1.0, 6.0, ((0, 32),))
    arrow_blocks = normal_values(streams_of[4], (TIMES, FE, NB), (NB * TIMES) ** -0.5, 0.03125, ((0, 4), (2, 32)))
    tip_right = normal_values(streams_of[5], (FE, R), 1.0, 6.0, (), jnp.float32)
    tip_inverse = normal_values(streams_of[6], (FE, FE), FE ** -0.5, 0.75, (), jnp.float32)
    return {"right_sides": right_sides, "diag_inverse": diag_inverse, "coupling": coupling, "carry_in": carry_in, "arrow_blocks": arrow_blocks, "tip_right": tip_right, "tip_inverse": tip_inverse}


def reference(right_sides, diag_inverse, coupling, carry_in, arrow_blocks, tip_right, tip_inverse):
    earlier = carry_in
    chain_rows = []
    arrow_sum = jnp.zeros((FE, R), jnp.float32)
    for block_no in range(TIMES):
        scaled = jnp.dot(diag_inverse[block_no], right_sides[block_no], preferred_element_type=jnp.float32)
        coupled = jnp.dot(coupling[block_no], earlier, preferred_element_type=jnp.float32)
        earlier = (scaled - coupled).astype(jnp.bfloat16)
        chain_rows.append(earlier)
        arrow_sum = arrow_sum + jnp.dot(arrow_blocks[block_no], earlier, preferred_element_type=jnp.float32)
    solution = jnp.dot(tip_inverse, tip_right - arrow_sum, precision=lax.Precision.HIGHEST, preferred_element_type=jnp.float32)
    return (jnp.stack(chain_rows, axis=0), solution)
```

```python
import functools

import jax
import jax.numpy as jnp
from jax import lax
from jax.experimental import pallas as pl
from jax.experimental.pallas import tpu as pltpu
from jax.sharding import PartitionSpec as P

MESH = pl.DeviceIdType.MESH
SIDE = 4
CHUNK = 32
AHEAD = 2


def device(x, y, z, core):
    return (lax.rem(x, SIDE), (lax.rem(y, SIDE) * SIDE + lax.rem(z, SIDE)) * 2 + core)


def times_transposed(rows, matrix):
    return lax.dot_general(
        rows, matrix, (((1,), (1,)), ((), ())), preferred_element_type=jnp.float32
    )


def kernel(
    rhs_ref, diag_ref, coup_ref, carry_ref, arrow_ref, tip_right_ref, tip_inverse_ref,
    out_ref, tip_ref,
    mats, own, gathered, arriving, part_a, part_b, send_a, send_b, recv_a, recv_b,
    state_a, state_b, arrow_own, turned, leaving, total, heard,
    mat_send, mat_recv, mat_local, sib_send, sib_recv,
    own_send, own_recv, vec_send, vec_recv, vec_local,
    a_send, a_recv, b_send, b_recv, next_send, next_recv,
    arrow_send, arrow_recv, out_send, out_recv, sum_send, sum_recv, tip_send, tip_recv,
):
    x = lax.axis_index("tm")
    place = lax.axis_index("mesh")
    y, z, core = place // (2 * SIDE), lax.rem(place // 2, SIDE), lax.rem(place, 2)
    other = 1 - core
    shard = rhs_ref.shape[1]
    chip = 2 * shard
    span = SIDE * chip
    lane = rhs_ref.shape[2] // 2
    chunks = lane // CHUNK
    sibling = device(x, y, z, other)
    along_z = lambda r: device(x, y, z + r, core)
    along_y = lambda r: device(x, y + r, z, core)
    along_x = lambda r: device(x + r, y, z, core)
    steps = range(1, SIDE)

    def aligned(value, unit):
        return pl.multiple_of(value, unit)

    def remote(src, dst, send, recv, target):
        return pltpu.make_async_remote_copy(
            src_ref=src, dst_ref=dst, send_sem=send, recv_sem=recv,
            device_id=target, device_id_type=MESH,
        )

    barrier = pltpu.get_barrier_semaphore()
    neighbours = [f(r) for f in (along_z, along_y, along_x) for r in steps] + [sibling]
    for target in neighbours:
        pl.semaphore_signal(barrier, inc=1, device_id=target, device_id_type=MESH)
    pl.semaphore_wait(barrier, len(neighbours))

    sources = (diag_ref.at[0], coup_ref.at[0], diag_ref.at[1], coup_ref.at[1])
    lines = (along_z, along_z, along_y, along_y)
    mine = (z, z, y, y)

    def block_of(m, at, half):
        return mats.at[m, pl.ds(aligned(at * chip + half * shard, shard), shard), :]

    def pieces(m, r):
        target_at = lax.rem(mine[m] + r, SIDE)
        rows = pl.ds(aligned(mine[m] * chip + core * shard, shard), shard)
        if m < 2:
            return [
                (
                    sources[m].at[:, pl.ds(aligned(a * span + target_at * chip, chip), chip)],
                    mats.at[m, rows, pl.ds(a * chip, chip)],
                )
                for a in range(SIDE)
            ]
        return [
            (
                sources[m].at[:, pl.ds(aligned(target_at * span, span), span)],
                mats.at[m, rows, :],
            )
        ]

    def send_matrix(m):
        for r in steps:
            for src, dst in pieces(m, r):
                remote(src, dst, mat_send.at[m, r], mat_recv.at[m, r], lines[m](r)).start()
        for src, dst in pieces(m, 0):
            remote(src, dst, sib_send.at[m, 0], sib_recv.at[m, 0], sibling).start()
            pltpu.make_async_copy(src, dst, mat_local.at[m]).start()

    def forward_copy(m, r):
        block = block_of(m, lax.rem(mine[m] - r + SIDE, SIDE), core)
        return remote(block, block, sib_send.at[m, r], sib_recv.at[m, r], sibling)

    def whole(m, r, half):
        return block_of(m, lax.rem(mine[m] - r + SIDE, SIDE), half)

    def arrive(*which):
        for r in (1, 3, 2):
            for m in which:
                remote(
                    whole(m, r, core), whole(m, r, core), mat_send.at[m, r], mat_recv.at[m, r], lines[m](r)
                ).wait_recv()
                forward_copy(m, r).start()
        for m in which:
            pltpu.make_async_copy(whole(m, 0, core), whole(m, 0, core), mat_local.at[m]).wait()
            for r in range(SIDE):
                remote(
                    whole(m, r, other), whole(m, r, other), sib_send.at[m, r], sib_recv.at[m, r], sibling
                ).wait_recv()

    send_matrix(0)
    send_matrix(1)

    vectors = (rhs_ref.at[0], carry_ref, rhs_ref.at[1])
    targets = (gathered.at[0], arriving, gathered.at[1])
    vec_lines = (along_y, along_y, along_z)
    vec_mine = (y, y, z)
    own_half = pl.ds(aligned(core * shard, shard), shard)

    def own_copy(v):
        return remote(
            turned.at[v], own.at[v, :, own_half], own_send.at[v], own_recv.at[v], sibling
        )

    def other_copy(v):
        half = own.at[v, :, pl.ds(aligned(other * shard, shard), shard)]
        return remote(half, half, own_send.at[v], own_recv.at[v], sibling)

    def turn(v):
        value = vectors[v][:, pl.ds(aligned(core * lane, lane), lane)]
        own[v, :, own_half] = value.T
        value = vectors[v][:, pl.ds(aligned(other * lane, lane), lane)]
        turned[v] = value.T
        own_copy(v).start()

    arrow_half = arrow_own.at[:, :, own_half]
    arrow_other = arrow_own.at[:, :, pl.ds(aligned(other * shard, shard), shard)]

    def vec_copy(v, r):
        slot = targets[v].at[:, pl.ds(aligned(vec_mine[v] * chip, chip), chip)]
        return remote(own.at[v], slot, vec_send.at[v, r], vec_recv.at[v, r], vec_lines[v](r))

    def vec_own(v):
        slot = targets[v].at[:, pl.ds(aligned(vec_mine[v] * chip, chip), chip)]
        return pltpu.make_async_copy(own.at[v], slot, vec_local.at[v])

    def vec_wait(v):
        for r in steps:
            at = lax.rem(vec_mine[v] - r + SIDE, SIDE)
            slot = targets[v].at[:, pl.ds(aligned(at * chip, chip), chip)]
            remote(slot, slot, vec_send.at[v, r], vec_recv.at[v, r], vec_lines[v](r)).wait_recv()
        vec_own(v).wait()

    def vec_start(v):
        other_copy(v).wait_recv()
        for r in steps:
            vec_copy(v, r).start()
        vec_own(v).start()

    turn(0)

    @pl.when(x == 0)
    def _():
        turn(1)

    turn(2)
    arrow_own[:, :, own_half] = arrow_ref[...]
    remote(arrow_ref, arrow_half, arrow_send, arrow_recv, sibling).start()
    vec_start(0)

    @pl.when(x == 0)
    def _():
        vec_start(1)

    vec_start(2)
    send_matrix(2)
    send_matrix(3)

    arrive(0, 1)
    vec_wait(0)
    part_a[...] = times_transposed(gathered[0], mats[0])

    @pl.when(x == 0)
    def _():
        vec_wait(1)

    def rows_of(k):
        return pl.ds(aligned(k * CHUNK, CHUNK), CHUNK)

    def chunk_copy(src, dst, send, recv, line, k, r):
        return remote(
            src.at[rows_of(k)], dst.at[r - 1, rows_of(k)], send.at[k, r], recv.at[k, r], line(r)
        )

    copy_a = functools.partial(chunk_copy, send_a, recv_a, a_send, a_recv, along_z)
    copy_b = functools.partial(chunk_copy, send_b, recv_b, b_send, b_recv, along_y)

    def copy_next(k):
        return remote(
            state_b.at[rows_of(k)], arriving.at[rows_of(k)], next_send.at[k], next_recv.at[k], along_x(1)
        )

    def spread(part, sent, matrix, source, copy, k):
        rows = rows_of(k)
        value = part[rows, :] - times_transposed(source[rows, :], matrix[...])
        part[rows, :] = value
        sent[rows, :] = value.astype(jnp.bfloat16)
        for r in (2, 1, 3):
            copy(k, r).start()

    def settle(part, received, state, copy, k):
        rows = rows_of(k)
        for r in (1, 3, 2):
            copy(k, r).wait_recv()
        value = part[rows, :]
        for r in steps:
            value = value + received[r - 1, rows, :].astype(jnp.float32)
        state[rows, :] = value.astype(jnp.bfloat16)

    def first(k):
        @pl.when(x > 0)
        def _():
            copy_next(k).wait_recv()

        spread(part_a, send_a, mats.at[1], arriving, copy_a, k)

    def second(k):
        settle(part_a, recv_a, state_a, copy_a, k)
        spread(part_b, send_b, mats.at[3], state_a, copy_b, k)

    def third(k):
        settle(part_b, recv_b, state_b, copy_b, k)

        @pl.when(x < SIDE - 1)
        def _():
            copy_next(k).start()

    def lead(k, carry):
        first(k)
        return carry

    lax.fori_loop(0, AHEAD, lead, 0)
    arrive(2, 3)
    vec_wait(2)
    part_b[...] = times_transposed(gathered[1], mats[2])

    def step(n, carry):
        @pl.when(n >= 2 * AHEAD)
        def _():
            third(n - 2 * AHEAD)

        @pl.when(n < chunks + AHEAD)
        def _():
            second(n - AHEAD)

        @pl.when(n < chunks)
        def _():
            first(n)

        return carry

    lax.fori_loop(AHEAD, chunks + 2 * AHEAD, step, 0)

    remote(arrow_other, arrow_other, arrow_send, arrow_recv, sibling).wait_recv()
    rows_a = pl.ds(aligned(z * chip, chip), chip)
    rows_b = pl.ds(aligned(y * chip, chip), chip)
    total[0] = times_transposed(arrow_own[0], state_a[:, rows_a]) + times_transposed(
        arrow_own[1], state_b[:, rows_b]
    )

    def sum_copy(phase, r):
        line = (along_z, along_y, along_x)[phase]
        return remote(
            total.at[phase], heard.at[phase, r - 1], sum_send.at[phase, r], sum_recv.at[phase, r], line(r)
        )

    def sum_wait(phase):
        for r in steps:
            sum_copy(phase, r).wait_recv()
        value = total[phase]
        for r in steps:
            value = value + heard[phase, r - 1]
        return value

    for r in steps:
        sum_copy(0, r).start()

    own_columns = pl.ds(aligned(core * lane, lane), lane)

    back = [(state_a, z), (state_b, y)]

    def out_copy(b, columns):
        return remote(
            leaving.at[b], out_ref.at[b, :, columns], out_send.at[b], out_recv.at[b], sibling
        )

    total[1] = sum_wait(0)
    for r in steps:
        sum_copy(1, r).start()

    for b, (state, at) in enumerate(back):
        start = at * chip
        leaving[b] = state[:, pl.ds(aligned(start + other * shard, shard), shard)].T
        out_copy(b, own_columns).start()
        out_ref[b, :, own_columns] = state[:, pl.ds(aligned(start + core * shard, shard), shard)].T

    total[2] = sum_wait(1)
    for r in steps:
        sum_copy(2, r).start()
    full = sum_wait(2)
    tip = jnp.dot(
        tip_inverse_ref[...],
        tip_right_ref[:, own_columns] - full,
        precision=lax.Precision.HIGHEST,
        preferred_element_type=jnp.float32,
    )
    total[3] = tip
    tip_copy = remote(total.at[3], tip_ref.at[:, own_columns], tip_send, tip_recv, sibling)
    tip_copy.start()
    tip_ref[:, own_columns] = tip

    for m in range(4):
        for r in steps:
            remote(whole(m, r, core), whole(m, r, core), mat_send.at[m, r], mat_recv.at[m, r], lines[m](r)).wait_send()
        for r in range(SIDE):
            forward_copy(m, r).wait_send()
    def vec_drain(v):
        own_copy(v).wait_send()
        for r in steps:
            vec_copy(v, r).wait_send()

    vec_drain(0)
    pl.when(x == 0)(lambda: vec_drain(1))
    vec_drain(2)

    remote(arrow_ref, arrow_half, arrow_send, arrow_recv, sibling).wait_send()

    def drain(k, carry):
        for r in steps:
            copy_a(k, r).wait_send()
            copy_b(k, r).wait_send()

        @pl.when(x < SIDE - 1)
        def _():
            copy_next(k).wait_send()

        return carry

    lax.fori_loop(0, chunks, drain, 0)
    for phase in range(3):
        for r in steps:
            sum_copy(phase, r).wait_send()
    other_columns = pl.ds(aligned(other * lane, lane), lane)
    for b in range(2):
        out_copy(b, own_columns).wait_send()
        out_copy(b, other_columns).wait_recv()
    tip_copy.wait_send()
    remote(total.at[3], tip_ref.at[:, other_columns], tip_send, tip_recv, sibling).wait_recv()


def body(right_sides, diag_inverse, coupling, carry_in, arrow_blocks, tip_right, tip_inverse):
    blocks, shard, columns = right_sides.shape
    effects = tip_right.shape[0]
    chip, span, lane = 2 * shard, 2 * shard * SIDE, columns // 2
    chunks = lane // CHUNK
    vmem = pl.BlockSpec(memory_space=pltpu.VMEM)
    hbm = pl.BlockSpec(memory_space=pl.ANY)
    half, full = jnp.bfloat16, jnp.float32
    dma = pltpu.SemaphoreType.DMA
    return pl.pallas_call(
        kernel,
        out_shape=(
            jax.ShapeDtypeStruct(right_sides.shape, half),
            jax.ShapeDtypeStruct(tip_right.shape, full),
        ),
        in_specs=[vmem, hbm, hbm, vmem, vmem, vmem, vmem],
        out_specs=(vmem, vmem),
        scratch_shapes=[
            pltpu.VMEM((4, span, span), half),
            pltpu.VMEM((3, lane, chip), half),
            pltpu.VMEM((2, lane, span), half),
            pltpu.VMEM((lane, span), half),
            pltpu.VMEM((lane, span), full),
            pltpu.VMEM((lane, span), full),
            pltpu.VMEM((lane, span), half),
            pltpu.VMEM((lane, span), half),
            pltpu.VMEM((SIDE - 1, lane, span), half),
            pltpu.VMEM((SIDE - 1, lane, span), half),
            pltpu.VMEM((lane, span), half),
            pltpu.VMEM((lane, span), half),
            pltpu.VMEM((blocks, effects, chip), half),
            pltpu.VMEM((3, lane, shard), half),
            pltpu.VMEM((blocks, shard, lane), half),
            pltpu.VMEM((4, effects, lane), full),
            pltpu.VMEM((3, SIDE - 1, effects, lane), full),
            dma((4, SIDE)), dma((4, SIDE)), dma((4,)), dma((4, SIDE)), dma((4, SIDE)),
            dma((3,)), dma((3,)), dma((3, SIDE)), dma((3, SIDE)), dma((3,)),
            dma((chunks, SIDE)), dma((chunks, SIDE)), dma((chunks, SIDE)), dma((chunks, SIDE)),
            dma((chunks,)), dma((chunks,)),
            dma, dma, dma((2,)), dma((2,)), dma((3, SIDE)), dma((3, SIDE)), dma, dma,
        ],
        compiler_params=pltpu.CompilerParams(
            collective_id=0, has_side_effects=True, vmem_limit_bytes=48 << 20
        ),
    )(right_sides, diag_inverse, coupling, carry_in, arrow_blocks, tip_right, tip_inverse)


def solution(mesh):
    placed = (
        P("tm", "mesh", None),
        P("tm", "mesh", None),
        P("tm", "mesh", None),
        P("mesh", None),
        P("tm", None, "mesh"),
        P(),
        P(),
    )
    return jax.shard_map(
        body, mesh=mesh, in_specs=placed, out_specs=(P("tm", "mesh", None), P()), check_vma=False
    )
```

```python
import functools

import jax
import jax.numpy as jnp
from jax import lax
from jax.experimental import pallas as pl
from jax.experimental.pallas import tpu as pltpu
from jax.sharding import PartitionSpec as P

MESH = pl.DeviceIdType.MESH
SIDE = 4
CHUNK = 16
VMEM_LIMIT = 63 << 20
AHEAD = 3


def device(x, y, z, core):
    return (lax.rem(x, SIDE), (lax.rem(y, SIDE) * SIDE + lax.rem(z, SIDE)) * 2 + core)


def times_transposed(rows, matrix):
    return lax.dot_general(
        rows, matrix, (((1,), (1,)), ((), ())), preferred_element_type=jnp.float32
    )


def kernel(
    rhs_hbm, diag_ref, coup_ref, carry_hbm, arrow_hbm, tip_right_hbm, tip_inverse_hbm,
    out_ref, tip_ref,
    rhs_ref, carry_ref, arrow_ref, tip_right_ref, tip_inverse_ref,
    mats, gathered, arriving, part_a, part_b, send_a, send_b, recv_a, recv_b,
    state_a, state_b, arrow_line, turned, leaving, line_sum, line_heard, plane_sum, plane_heard,
    load_sem, mat_send, mat_recv, mat_local, sib_send, sib_recv,
    turn_send, turn_recv, vec_send, vec_recv,
    a_send, a_recv, b_send, b_recv, next_send, next_recv,
    arrow_sib_send, arrow_sib_recv, arrow_send, arrow_recv, arrow_local,
    out_send, out_recv, line_send, line_recv, plane_send, plane_recv,
):
    x = lax.axis_index("tm")
    place = lax.axis_index("mesh")
    y, z, core = place // (2 * SIDE), lax.rem(place // 2, SIDE), lax.rem(place, 2)
    other = 1 - core
    shard = rhs_ref.shape[1]
    chip = 2 * shard
    span = SIDE * chip
    lane = rhs_ref.shape[2] // 2
    chunks = lane // CHUNK
    effects = tip_ref.shape[0]
    sibling = device(x, y, z, other)
    along_z = lambda r: device(x, y, z + r, core)
    along_y = lambda r: device(x, y + r, z, core)
    along_x = lambda r: device(x + r, y, z, core)
    across_x = lambda r: device(x + r, y, z, other)
    steps = range(1, SIDE)

    loads = [
        pltpu.make_async_copy(src, dst, load_sem.at[i])
        for i, (src, dst) in enumerate((
            (rhs_hbm, rhs_ref), (carry_hbm, carry_ref), (arrow_hbm, arrow_ref),
            (tip_right_hbm, tip_right_ref), (tip_inverse_hbm, tip_inverse_ref),
        ))
    ]
    for load in loads:
        load.start()

    def aligned(value, unit):
        return pl.multiple_of(value, unit)

    def remote(src, dst, send, recv, target):
        return pltpu.make_async_remote_copy(
            src_ref=src, dst_ref=dst, send_sem=send, recv_sem=recv,
            device_id=target, device_id_type=MESH,
        )

    barrier = pltpu.get_barrier_semaphore()
    neighbours = [f(r) for f in (along_z, along_y, along_x, across_x) for r in steps]
    neighbours.append(sibling)
    for target in neighbours:
        pl.semaphore_signal(barrier, inc=1, device_id=target, device_id_type=MESH)

    vectors = (lambda: rhs_ref[0], lambda: carry_ref[...], lambda: rhs_ref[1])
    targets = (gathered.at[0], arriving, gathered.at[1])
    vec_lines = (along_y, along_y, along_z)
    vec_mine = (y, y, z)

    def slot(v, at, half):
        return targets[v].at[:, pl.ds(aligned(at * chip + half * shard, shard), shard)]

    def turn(v):
        value = vectors[v]().T
        mine = jnp.where(core == 0, value[:lane], value[lane:])
        slot(v, vec_mine[v], core)[...] = mine
        turned[v] = jnp.where(core == 0, value[lane:], value[:lane])

    loads[0].wait()
    loads[1].wait()
    turn(0)

    @pl.when(x == 0)
    def _():
        turn(1)

    turn(2)
    pl.semaphore_wait(barrier, len(neighbours))

    sources = (diag_ref.at[0], coup_ref.at[0], diag_ref.at[1], coup_ref.at[1])
    lines = (along_z, along_z, along_y, along_y)
    mine = (z, z, y, y)

    def pieces(m, r):
        target_at = lax.rem(mine[m] + r, SIDE)
        rows = pl.ds(aligned(mine[m] * chip + core * shard, shard), shard)
        if m < 2:
            return [
                (
                    sources[m].at[:, pl.ds(aligned(a * span + target_at * chip, chip), chip)],
                    mats.at[m, rows, pl.ds(a * chip, chip)],
                )
                for a in range(SIDE)
            ]
        return [
            (
                sources[m].at[:, pl.ds(aligned(target_at * span, span), span)],
                mats.at[m, rows, :],
            )
        ]

    def send_matrix(m):
        for r in (2, 1, 3):
            for src, dst in pieces(m, r):
                remote(src, dst, mat_send.at[m, r], mat_recv.at[m, r], lines[m](r)).start()

    def send_local(m):
        for src, dst in pieces(m, 0):
            remote(src, dst, sib_send.at[m, 0], sib_recv.at[m, 0], sibling).start()
            pltpu.make_async_copy(src, dst, mat_local.at[m]).start()

    def block(m, r, half):
        at = lax.rem(mine[m] - r + SIDE, SIDE)
        return mats.at[m, pl.ds(aligned(at * chip + half * shard, shard), shard), :]

    def line_copy(m, r):
        rows = block(m, r, core)
        return remote(rows, rows, mat_send.at[m, r], mat_recv.at[m, r], lines[m](r))

    def sibling_copy(m, r, half):
        rows = block(m, r, half)
        return remote(rows, rows, sib_send.at[m, r], sib_recv.at[m, r], sibling)

    def forward(m):
        for r in (1, 3, 2):
            line_copy(m, r).wait_recv()
            sibling_copy(m, r, core).start()

    def complete(m):
        rows = block(m, 0, core)
        pltpu.make_async_copy(rows, rows, mat_local.at[m]).wait()
        for r in range(SIDE):
            sibling_copy(m, r, other).wait_recv()

    def turn_copy(v):
        return remote(
            turned.at[v], slot(v, vec_mine[v], core), turn_send.at[v], turn_recv.at[v], sibling
        )

    def vec_copy(v, r, half):
        rows = slot(v, vec_mine[v], half)
        return remote(
            rows, rows, vec_send.at[v, r, half], vec_recv.at[v, r, half], vec_lines[v](r)
        )

    def vec_begin(v):
        turn_copy(v).start()
        for r in (2, 1, 3):
            vec_copy(v, r, core).start()

    def vec_rest(v):
        rows = slot(v, vec_mine[v], other)
        remote(rows, rows, turn_send.at[v], turn_recv.at[v], sibling).wait_recv()
        for r in (2, 1, 3):
            vec_copy(v, r, other).start()

    def vec_wait(v):
        for r in (1, 3, 2):
            for half in range(2):
                rows = slot(v, lax.rem(vec_mine[v] - r + SIDE, SIDE), half)
                remote(
                    rows, rows, vec_send.at[v, r, half], vec_recv.at[v, r, half], vec_lines[v](r)
                ).wait_recv()

    arrow_lines = (along_z, along_y)
    arrow_mine = (z, y)

    def arrow_slot(b, at, half):
        return arrow_line.at[b, :, pl.ds(aligned(at * chip + half * shard, shard), shard)]

    def arrow_local_copy(b):
        return pltpu.make_async_copy(
            arrow_ref.at[b], arrow_slot(b, arrow_mine[b], core), arrow_local.at[b]
        )

    def arrow_sibling_copy(b, half):
        return remote(
            arrow_ref.at[b], arrow_slot(b, arrow_mine[b], half),
            arrow_sib_send.at[b], arrow_sib_recv.at[b], sibling,
        )

    def arrow_copy(b, r, at):
        rows = arrow_line.at[b, :, pl.ds(aligned(at * chip, chip), chip)]
        return remote(rows, rows, arrow_send.at[b, r], arrow_recv.at[b, r], arrow_lines[b](r))

    vec_begin(0)

    @pl.when(x == 0)
    def _():
        vec_begin(1)

    send_matrix(0)
    send_matrix(1)
    turn_copy(2).start()
    send_local(0)
    send_local(1)
    vec_rest(0)

    @pl.when(x == 0)
    def _():
        vec_rest(1)

    send_matrix(2)
    send_matrix(3)
    send_local(2)
    send_local(3)
    loads[2].wait()
    for b in range(2):
        arrow_local_copy(b).start()
        arrow_sibling_copy(b, core).start()

    forward(0)
    vec_wait(0)
    complete(0)
    part_a[...] = times_transposed(gathered[0], mats[0])
    forward(1)
    for r in (2, 1, 3):
        vec_copy(2, r, core).start()
    vec_rest(2)
    complete(1)

    @pl.when(x == 0)
    def _():
        vec_wait(1)

    def rows_of(k):
        return pl.ds(aligned(k * CHUNK, CHUNK), CHUNK)

    def chunk_copy(src, dst, send, recv, line, k, r):
        return remote(
            src.at[rows_of(k)], dst.at[r - 1, rows_of(k)], send.at[k, r], recv.at[k, r], line(r)
        )

    copy_a = functools.partial(chunk_copy, send_a, recv_a, a_send, a_recv, along_z)
    copy_b = functools.partial(chunk_copy, send_b, recv_b, b_send, b_recv, along_y)

    def copy_next(k):
        return remote(
            state_b.at[rows_of(k)], arriving.at[rows_of(k)], next_send.at[k], next_recv.at[k], along_x(1)
        )

    def spread(part, sent, matrix, source, copy, k):
        rows = rows_of(k)
        value = part[rows, :] - times_transposed(source[rows, :], matrix[...])
        part[rows, :] = value
        sent[rows, :] = value.astype(jnp.bfloat16)
        for r in (2, 1, 3):
            copy(k, r).start()

    def settle(part, received, state, copy, k):
        rows = rows_of(k)
        for r in (1, 3, 2):
            copy(k, r).wait_recv()
        value = part[rows, :]
        for r in steps:
            value = value + received[r - 1, rows, :].astype(jnp.float32)
        state[rows, :] = value.astype(jnp.bfloat16)

    def first(k):
        @pl.when(x > 0)
        def _():
            copy_next(k).wait_recv()

        spread(part_a, send_a, mats.at[1], arriving, copy_a, k)

    def second(k):
        settle(part_a, recv_a, state_a, copy_a, k)
        spread(part_b, send_b, mats.at[3], state_a, copy_b, k)

    def third(k):
        settle(part_b, recv_b, state_b, copy_b, k)

        @pl.when(x < SIDE - 1)
        def _():
            copy_next(k).start()

    def second_block():
        forward(2)
        forward(3)
        vec_wait(2)
        complete(2)
        part_b[...] = times_transposed(gathered[1], mats[2])
        complete(3)
        for b in range(2):
            arrow_sibling_copy(b, other).wait_recv()
            arrow_local_copy(b).wait()
            for r in steps:
                arrow_copy(b, r, arrow_mine[b]).start()

    pl.when(x > 0)(second_block)

    def lead(k, carry):
        first(k)
        return carry

    lax.fori_loop(0, AHEAD, lead, 0)
    pl.when(x == 0)(second_block)

    def step(n, carry):
        @pl.when(n >= 2 * AHEAD)
        def _():
            third(n - 2 * AHEAD)

        @pl.when(jnp.logical_and(n >= AHEAD, n < chunks + AHEAD))
        def _():
            second(n - AHEAD)

        @pl.when(n < chunks)
        def _():
            first(n)

        return carry

    sum_lines = (along_y, along_z)
    half_lane = lane // 2

    def line_copy_of(b, h, r):
        return remote(
            line_sum.at[b, h], line_heard.at[b, h, r - 1],
            line_send.at[b, h, r], line_recv.at[b, h, r], sum_lines[b](r),
        )

    def line_begin(b, h):
        state = (state_a, state_b)[b]
        line_sum[b, h] = times_transposed(
            arrow_line[b], state[pl.ds(h * half_lane, half_lane), :]
        )
        for r in (2, 1, 3):
            line_copy_of(b, h, r).start()

    def plane_targets(h):
        found = []
        for r in range(SIDE):
            if r:
                found.append((0, r, along_x(r)))
            found.append((1, r, across_x(r) if r else sibling))
        return [
            remote(
                plane_sum.at[h], plane_heard.at[h, cross, r],
                plane_send.at[h, cross, r], plane_recv.at[h, cross, r], target,
            )
            for cross, r, target in found
        ]

    def plane_begin(h):
        value = jnp.zeros((effects, half_lane), jnp.float32)
        for b in range(2):
            value = value + line_sum[b, h]
            for r in steps:
                line_copy_of(b, h, r).wait_recv()
                value = value + line_heard[b, h, r - 1]
        plane_sum[h] = value
        for copy in plane_targets(h):
            copy.start()

    middle = chunks // 2 + 2 * AHEAD
    lax.fori_loop(AHEAD, middle, step, 0)
    for b in range(2):
        for r in steps:
            arrow_copy(b, r, lax.rem(arrow_mine[b] - r + SIDE, SIDE)).wait_recv()
    line_begin(0, 0)
    line_begin(1, 0)
    lax.fori_loop(middle, chunks + 2 * AHEAD, step, 0)
    line_begin(1, 1)
    line_begin(0, 1)
    plane_begin(0)

    def out_copy(b, columns):
        return remote(
            leaving.at[b], out_ref.at[b, :, columns], out_send.at[b], out_recv.at[b], sibling
        )

    own_columns = pl.ds(aligned(core * lane, lane), lane)
    other_columns = pl.ds(aligned(other * lane, lane), lane)
    for b, (state, at) in enumerate([(state_a, z), (state_b, y)]):
        start = at * chip
        leaving[b] = state[:, pl.ds(aligned(start + other * shard, shard), shard)].T
        out_copy(b, own_columns).start()
        out_ref[b, :, own_columns] = state[:, pl.ds(aligned(start + core * shard, shard), shard)].T

    plane_begin(1)

    for m in range(4):
        for r in steps:
            line_copy(m, r).wait_send()
        for r in range(SIDE):
            sibling_copy(m, r, core).wait_send()

    def vec_drain(v):
        turn_copy(v).wait_send()
        for r in steps:
            for half in range(2):
                vec_copy(v, r, half).wait_send()

    vec_drain(0)
    pl.when(x == 0)(lambda: vec_drain(1))
    vec_drain(2)
    for b in range(2):
        arrow_sibling_copy(b, core).wait_send()
        for r in steps:
            arrow_copy(b, r, arrow_mine[b]).wait_send()

    def drain(k, carry):
        for r in steps:
            copy_a(k, r).wait_send()
            copy_b(k, r).wait_send()

        @pl.when(x < SIDE - 1)
        def _():
            copy_next(k).wait_send()

        return carry

    lax.fori_loop(0, chunks, drain, 0)
    for b in range(2):
        out_copy(b, own_columns).wait_send()
        out_copy(b, other_columns).wait_recv()
        for h in range(2):
            for r in steps:
                line_copy_of(b, h, r).wait_send()
    loads[3].wait()
    loads[4].wait()

    for h in range(2):
        for copy in plane_targets(h):
            copy.wait_send()
            copy.wait_recv()
        for cross, owner in enumerate((core, other)):
            value = plane_heard[h, 1, 0] if cross else plane_sum[h]
            for r in steps:
                value = value + plane_heard[h, cross, r]
            columns = pl.ds(aligned(owner * lane + h * half_lane, half_lane), half_lane)
            tip_ref[:, columns] = jnp.dot(
                tip_inverse_ref[...],
                tip_right_ref[:, columns] - value,
                precision=lax.Precision.HIGHEST,
                preferred_element_type=jnp.float32,
            )


def body(right_sides, diag_inverse, coupling, carry_in, arrow_blocks, tip_right, tip_inverse):
    blocks, shard, columns = right_sides.shape
    effects = tip_right.shape[0]
    chip, span, lane = 2 * shard, 2 * shard * SIDE, columns // 2
    chunks = lane // CHUNK
    vmem = pl.BlockSpec(memory_space=pltpu.VMEM)
    hbm = pl.BlockSpec(memory_space=pl.ANY)
    half, full = jnp.bfloat16, jnp.float32
    dma = pltpu.SemaphoreType.DMA
    return pl.pallas_call(
        kernel,
        out_shape=(
            jax.ShapeDtypeStruct(right_sides.shape, half),
            jax.ShapeDtypeStruct(tip_right.shape, full),
        ),
        in_specs=[hbm] * 7,
        out_specs=(vmem, vmem),
        scratch_shapes=[
            pltpu.VMEM(right_sides.shape, half),
            pltpu.VMEM(carry_in.shape, half),
            pltpu.VMEM(arrow_blocks.shape, half),
            pltpu.VMEM(tip_right.shape, full),
            pltpu.VMEM(tip_inverse.shape, full),
            pltpu.VMEM((4, span, span), half),
            pltpu.VMEM((2, lane, span), half),
            pltpu.VMEM((lane, span), half),
            pltpu.VMEM((lane, span), full),
            pltpu.VMEM((lane, span), full),
            pltpu.VMEM((lane, span), half),
            pltpu.VMEM((lane, span), half),
            pltpu.VMEM((SIDE - 1, lane, span), half),
            pltpu.VMEM((SIDE - 1, lane, span), half),
            pltpu.VMEM((lane, span), half),
            pltpu.VMEM((lane, span), half),
            pltpu.VMEM((blocks, effects, span), half),
            pltpu.VMEM((3, lane, shard), half),
            pltpu.VMEM((blocks, shard, lane), half),
            pltpu.VMEM((2, 2, effects, lane // 2), full),
            pltpu.VMEM((2, 2, SIDE - 1, effects, lane // 2), full),
            pltpu.VMEM((2, effects, lane // 2), full),
            pltpu.VMEM((2, 2, SIDE, effects, lane // 2), full),
            dma((5,)), dma((4, SIDE)), dma((4, SIDE)), dma((4,)), dma((4, SIDE)), dma((4, SIDE)),
            dma((3,)), dma((3,)), dma((3, SIDE, 2)), dma((3, SIDE, 2)),
            dma((chunks, SIDE)), dma((chunks, SIDE)), dma((chunks, SIDE)), dma((chunks, SIDE)),
            dma((chunks,)), dma((chunks,)),
            dma((2,)), dma((2,)), dma((2, SIDE)), dma((2, SIDE)), dma((2,)),
            dma((2,)), dma((2,)), dma((2, 2, SIDE)), dma((2, 2, SIDE)), dma((2, 2, SIDE)), dma((2, 2, SIDE)),
        ],
        compiler_params=pltpu.CompilerParams(
            collective_id=0, has_side_effects=True, vmem_limit_bytes=VMEM_LIMIT
        ),
    )(right_sides, diag_inverse, coupling, carry_in, arrow_blocks, tip_right, tip_inverse)


def solution(mesh):
    placed = (
        P("tm", "mesh", None),
        P("tm", "mesh", None),
        P("tm", "mesh", None),
        P("mesh", None),
        P("tm", None, "mesh"),
        P(),
        P(),
    )
    return jax.shard_map(
        body, mesh=mesh, in_specs=placed, out_specs=(P("tm", "mesh", None), P()), check_vma=False
    )
```

```python
import functools

import jax
import jax.numpy as jnp
from jax import lax
from jax.experimental import pallas as pl
from jax.experimental.pallas import tpu as pltpu
from jax.sharding import PartitionSpec as P

MESH = pl.DeviceIdType.MESH
SIDE = 4
CHUNK = 16
VMEM_LIMIT = 63 << 20
AHEAD = 4


def device(x, y, z, core):
    return (lax.rem(x, SIDE), (lax.rem(y, SIDE) * SIDE + lax.rem(z, SIDE)) * 2 + core)


def times_transposed(rows, matrix):
    return lax.dot_general(
        rows, matrix, (((1,), (1,)), ((), ())), preferred_element_type=jnp.float32
    )


def kernel(
    rhs_hbm, diag_ref, coup_ref, carry_hbm, arrow_hbm, tip_right_hbm, tip_inverse_hbm,
    out_ref, tip_ref,
    rhs_ref, carry_ref, arrow_ref, tip_right_ref, tip_inverse_ref,
    mats, gathered, arriving, part_a, part_b, send_a, send_b, recv_a, recv_b,
    state_a, state_b, flipped, relay, relay_carry, arrow_line, turned, leaving, line_sum, line_heard, plane_sum, plane_heard,
    load_sem, mat_send, mat_recv, mat_local, sib_send, sib_recv,
    relay_recv, relay_send, carry_recv, carry_send,
    turn_send, turn_recv, vec_send, vec_recv,
    a_send, a_recv, b_send, b_recv, next_send, next_recv,
    arrow_sib_send, arrow_sib_recv, arrow_send, arrow_recv, arrow_local,
    out_send, out_recv, line_send, line_recv, plane_send, plane_recv,
):
    x = lax.axis_index("tm")
    place = lax.axis_index("mesh")
    y, z, core = place // (2 * SIDE), lax.rem(place // 2, SIDE), lax.rem(place, 2)
    other = 1 - core
    shard = rhs_ref.shape[1]
    chip = 2 * shard
    span = SIDE * chip
    lane = rhs_ref.shape[2] // 2
    chunks = lane // CHUNK
    effects = tip_ref.shape[0]
    sibling = device(x, y, z, other)
    along_z = lambda r: device(x, y, z + r, core)
    along_y = lambda r: device(x, y + r, z, core)
    along_x = lambda r: device(x + r, y, z, core)
    across_x = lambda r: device(x + r, y, z, other)
    steps = range(1, SIDE)

    loads = [
        pltpu.make_async_copy(src, dst, load_sem.at[i])
        for i, (src, dst) in enumerate((
            (rhs_hbm, rhs_ref), (carry_hbm, carry_ref), (arrow_hbm, arrow_ref),
            (tip_right_hbm, tip_right_ref), (tip_inverse_hbm, tip_inverse_ref),
        ))
    ]
    for load in loads:
        load.start()

    helper = jnp.logical_or(x == 1, x == 3)
    part = x // 2

    def aligned(value, unit):
        return pl.multiple_of(value, unit)

    def remote(src, dst, send, recv, target):
        return pltpu.make_async_remote_copy(
            src_ref=src, dst_ref=dst, send_sem=send, recv_sem=recv,
            device_id=target, device_id_type=MESH,
        )

    barrier = pltpu.get_barrier_semaphore()
    neighbours = [f(r) for f in (along_z, along_y, along_x, across_x) for r in steps]
    neighbours += [sibling]
    neighbours += [device(x + d, y + a, z + b, core) for d in (1, 3) for a, b in ((0, 2), (2, 0))]
    for target in neighbours:
        pl.semaphore_signal(barrier, inc=1, device_id=target, device_id_type=MESH)

    half_lane = lane // 2
    targets = (gathered.at[0], relay_carry, gathered.at[1])
    vec_lines = (along_y, along_y, along_z)
    vec_mine = (y, y, z)

    def slot(v, at, half):
        return targets[v].at[:, pl.ds(aligned(at * chip + half * shard, shard), shard)]

    def leaves(v):
        return turned.at[v, pl.ds(0, half_lane)] if v == 1 else turned.at[v]

    def turn(v, value):
        value = value.T
        mine, theirs = value[:lane], value[lane:]
        if v == 1:
            mine = jnp.where(part == 0, mine[:half_lane], mine[half_lane:])
            theirs = jnp.where(part == 0, theirs[:half_lane], theirs[half_lane:])
        mine, theirs = jnp.where(core == 0, mine, theirs), jnp.where(core == 0, theirs, mine)
        slot(v, vec_mine[v], core)[...] = mine
        leaves(v)[...] = theirs

    loads[0].wait()
    loads[1].wait()
    turn(0, rhs_ref[0])
    pl.when(helper)(lambda: turn(1, carry_ref[...]))
    turn(2, rhs_ref[1])
    pl.semaphore_wait(barrier, len(neighbours))

    sources = (diag_ref.at[0], coup_ref.at[0], diag_ref.at[1], coup_ref.at[1])
    lines = (along_z, along_z, along_y, along_y)
    mine = (z, z, y, y)

    def pieces(m, r):
        target_at = lax.rem(mine[m] + r, SIDE)
        rows = pl.ds(aligned(mine[m] * chip + core * shard, shard), shard)
        if m < 2:
            return [
                (
                    sources[m].at[:, pl.ds(aligned(a * span + target_at * chip, chip), chip)],
                    mats.at[m, rows, pl.ds(a * chip, chip)],
                )
                for a in range(SIDE)
            ]
        return [
            (
                sources[m].at[:, pl.ds(aligned(target_at * span, span), span)],
                mats.at[m, rows, :],
            )
        ]

    def send_near(m):
        for r in (1, 3):
            for src, dst in pieces(m, r):
                remote(src, dst, mat_send.at[m, r], mat_recv.at[m, r], lines[m](r)).start()

    def send_far(m):
        for src, dst in pieces(m, 2):
            remote(src, dst, mat_send.at[m, 2], mat_recv.at[m, 2], lines[m](2)).start()

    def send_round(m):
        rows = shard // 2
        found = pieces(m, 2)
        width = span // len(found)
        for n, (src, _) in enumerate(found):
            columns = pl.ds(n * width, width)
            for h, d in enumerate((1, 3)):
                target = device(x + d, y, z + 2, core) if m < 2 else device(x + d, y + 2, z, core)
                remote(
                    src.at[pl.ds(h * rows, rows)], relay.at[m, :, columns],
                    mat_send.at[m, 2], relay_recv.at[m], target,
                ).start()

    def pass_on(m):
        rows = shard // 2
        at = lax.rem(mine[m] + 2, SIDE)
        dst = mats.at[m, pl.ds(aligned(at * chip + core * shard + part * rows, rows), rows), :]
        return remote(relay.at[m], dst, relay_send.at[m], mat_recv.at[m, 2], device(0, y, z, core))

    def relay_wait(m):
        remote(relay.at[m], relay.at[m], relay_send.at[m], relay_recv.at[m], device(0, y, z, core)).wait_recv()

    def send_local(m):
        for src, dst in pieces(m, 0):
            remote(src, dst, sib_send.at[m, 0], sib_recv.at[m, 0], sibling).start()
            pltpu.make_async_copy(src, dst, mat_local.at[m]).start()

    def block(m, r, half):
        at = lax.rem(mine[m] - r + SIDE, SIDE)
        return mats.at[m, pl.ds(aligned(at * chip + half * shard, shard), shard), :]

    def line_copy(m, r):
        rows = block(m, r, core)
        return remote(rows, rows, mat_send.at[m, r], mat_recv.at[m, r], lines[m](r))

    def sibling_copy(m, r, half):
        rows = block(m, r, half)
        return remote(rows, rows, sib_send.at[m, r], sib_recv.at[m, r], sibling)

    def flip(m, r, half):
        if m % 2:
            at = lax.rem(mine[m] - r + SIDE, SIDE)
            columns = pl.ds(aligned(at * chip + half * shard, shard), shard)
            flipped[m // 2, :, columns] = block(m, r, half)[...].T

    def forward(m):
        for r in (1, 3, 2):
            line_copy(m, r).wait_recv()
            sibling_copy(m, r, core).start()
            flip(m, r, core)

    def complete(m):
        rows = block(m, 0, core)
        pltpu.make_async_copy(rows, rows, mat_local.at[m]).wait()
        flip(m, 0, core)
        for r in (0, 1, 3, 2):
            sibling_copy(m, r, other).wait_recv()
            flip(m, r, other)

    def turn_copy(v):
        return remote(
            leaves(v), slot(v, vec_mine[v], core), turn_send.at[v], turn_recv.at[v], sibling
        )

    def vec_copy(v, r, half):
        rows = slot(v, vec_mine[v], half)
        return remote(
            rows, rows, vec_send.at[v, r, half], vec_recv.at[v, r, half], vec_lines[v](r)
        )

    def vec_begin(v):
        turn_copy(v).start()
        for r in (2, 1, 3):
            vec_copy(v, r, core).start()

    def vec_rest(v):
        rows = slot(v, vec_mine[v], other)
        remote(rows, rows, turn_send.at[v], turn_recv.at[v], sibling).wait_recv()
        for r in (2, 1, 3):
            vec_copy(v, r, other).start()

    def vec_wait(v):
        for r in (1, 3, 2):
            for half in range(2):
                rows = slot(v, lax.rem(vec_mine[v] - r + SIDE, SIDE), half)
                remote(
                    rows, rows, vec_send.at[v, r, half], vec_recv.at[v, r, half], vec_lines[v](r)
                ).wait_recv()

    arrow_lines = (along_z, along_y)
    arrow_mine = (z, y)

    def arrow_slot(b, at, half):
        return arrow_line.at[b, :, pl.ds(aligned(at * chip + half * shard, shard), shard)]

    def arrow_local_copy(b):
        return pltpu.make_async_copy(
            arrow_ref.at[b], arrow_slot(b, arrow_mine[b], core), arrow_local.at[b]
        )

    def arrow_sibling_copy(b, half):
        return remote(
            arrow_ref.at[b], arrow_slot(b, arrow_mine[b], half),
            arrow_sib_send.at[b], arrow_sib_recv.at[b], sibling,
        )

    def arrow_copy(b, r, at):
        rows = arrow_line.at[b, :, pl.ds(aligned(at * chip, chip), chip)]
        return remote(rows, rows, arrow_send.at[b, r], arrow_recv.at[b, r], arrow_lines[b](r))

    vec_begin(0)
    pl.when(helper)(lambda: vec_begin(1))
    for m in range(2):
        send_near(m)

    @pl.when(x == 0)
    def _():
        for m in range(2):
            send_round(m)

    turn_copy(2).start()
    vec_rest(0)
    pl.when(helper)(lambda: vec_rest(1))
    for m in range(2, 4):
        send_near(m)

    @pl.when(x == 0)
    def _():
        for m in range(2, 4):
            send_round(m)

    for m in range(4):
        send_local(m)

    def carry_copy(p):
        return remote(
            relay_carry, arriving.at[pl.ds(p * half_lane, half_lane)],
            carry_send, carry_recv.at[p], device(0, y, z, core),
        )

    @pl.when(helper)
    def _():
        for m in range(2):
            relay_wait(m)
            pass_on(m).start()
        vec_wait(1)
        for p in range(2):
            pl.when(part == p)(carry_copy(p).start)
        for m in range(2, 4):
            relay_wait(m)
            pass_on(m).start()

    @pl.when(x > 0)
    def _():
        for m in range(4):
            send_far(m)

    loads[2].wait()
    for b in range(2):
        arrow_local_copy(b).start()
        arrow_sibling_copy(b, core).start()

    forward(0)
    vec_wait(0)
    complete(0)
    part_a[...] = times_transposed(gathered[0], mats[0])
    forward(1)
    for r in (2, 1, 3):
        vec_copy(2, r, core).start()
    vec_rest(2)
    complete(1)

    @pl.when(x == 0)
    def _():
        for p in range(2):
            carry_copy(p).wait_recv()

    def rows_of(k):
        return pl.ds(aligned(k * CHUNK, CHUNK), CHUNK)

    def chunk_copy(src, dst, send, recv, line, k, r):
        return remote(
            src.at[rows_of(k)], dst.at[r - 1, rows_of(k)], send.at[k, r], recv.at[k, r], line(r)
        )

    copy_a = functools.partial(chunk_copy, send_a, recv_a, a_send, a_recv, along_z)
    copy_b = functools.partial(chunk_copy, send_b, recv_b, b_send, b_recv, along_y)

    def copy_next(k):
        return remote(
            state_b.at[rows_of(k)], arriving.at[rows_of(k)], next_send.at[k], next_recv.at[k], along_x(1)
        )

    def spread(terms, sent, matrix, source, copy, k):
        rows = rows_of(k)
        value = terms[rows, :] - jnp.dot(
            source[rows, :], matrix[...], preferred_element_type=jnp.float32
        )
        terms[rows, :] = value
        sent[rows, :] = value.astype(jnp.bfloat16)
        for r in (2, 1, 3):
            copy(k, r).start()

    def settle(terms, received, state, copy, k):
        rows = rows_of(k)
        for r in (1, 3, 2):
            copy(k, r).wait_recv()
        value = terms[rows, :]
        for r in steps:
            value = value + received[r - 1, rows, :].astype(jnp.float32)
        state[rows, :] = value.astype(jnp.bfloat16)

    def first(k):
        @pl.when(x > 0)
        def _():
            copy_next(k).wait_recv()

        spread(part_a, send_a, flipped.at[0], arriving, copy_a, k)

    def second(k):
        settle(part_a, recv_a, state_a, copy_a, k)
        spread(part_b, send_b, flipped.at[1], state_a, copy_b, k)

    def third(k):
        settle(part_b, recv_b, state_b, copy_b, k)

        @pl.when(x < SIDE - 1)
        def _():
            copy_next(k).start()

    def second_block():
        forward(2)
        forward(3)
        vec_wait(2)
        complete(2)
        part_b[...] = times_transposed(gathered[1], mats[2])
        complete(3)
        for b in range(2):
            arrow_sibling_copy(b, other).wait_recv()
            arrow_local_copy(b).wait()
            for r in steps:
                arrow_copy(b, r, arrow_mine[b]).start()

    pl.when(x > 0)(second_block)

    def lead(k, carry):
        first(k)
        return carry

    lax.fori_loop(0, AHEAD, lead, 0)
    pl.when(x == 0)(second_block)

    def step(n, carry):
        @pl.when(n >= 2 * AHEAD)
        def _():
            third(n - 2 * AHEAD)

        @pl.when(jnp.logical_and(n >= AHEAD, n < chunks + AHEAD))
        def _():
            second(n - AHEAD)

        @pl.when(n < chunks)
        def _():
            first(n)

        return carry

    sum_lines = (along_y, along_z)

    def line_copy_of(b, h, r):
        return remote(
            line_sum.at[b, h], line_heard.at[b, h, r - 1],
            line_send.at[b, h, r], line_recv.at[b, h, r], sum_lines[b](r),
        )

    def line_begin(b, h):
        state = (state_a, state_b)[b]
        line_sum[b, h] = times_transposed(
            arrow_line[b], state[pl.ds(h * half_lane, half_lane), :]
        )
        for r in (2, 1, 3):
            line_copy_of(b, h, r).start()

    def plane_targets(h):
        found = []
        for r in range(SIDE):
            if r:
                found.append((0, r, along_x(r)))
            found.append((1, r, across_x(r) if r else sibling))
        return [
            remote(
                plane_sum.at[h], plane_heard.at[h, cross, r],
                plane_send.at[h, cross, r], plane_recv.at[h, cross, r], target,
            )
            for cross, r, target in found
        ]

    def plane_begin(h):
        value = jnp.zeros((effects, half_lane), jnp.float32)
        for b in range(2):
            value = value + line_sum[b, h]
            for r in steps:
                line_copy_of(b, h, r).wait_recv()
                value = value + line_heard[b, h, r - 1]
        plane_sum[h] = value
        for copy in plane_targets(h):
            copy.start()

    middle = chunks // 2 + 2 * AHEAD
    lax.fori_loop(AHEAD, middle, step, 0)
    for b in range(2):
        for r in steps:
            arrow_copy(b, r, lax.rem(arrow_mine[b] - r + SIDE, SIDE)).wait_recv()
    line_begin(0, 0)
    line_begin(1, 0)
    lax.fori_loop(middle, chunks + 2 * AHEAD, step, 0)
    line_begin(1, 1)
    line_begin(0, 1)
    plane_begin(0)

    def out_copy(b, columns):
        return remote(
            leaving.at[b], out_ref.at[b, :, columns], out_send.at[b], out_recv.at[b], sibling
        )

    own_columns = pl.ds(aligned(core * lane, lane), lane)
    other_columns = pl.ds(aligned(other * lane, lane), lane)
    for b, (state, at) in enumerate([(state_a, z), (state_b, y)]):
        start = at * chip
        leaving[b] = state[:, pl.ds(aligned(start + other * shard, shard), shard)].T
        out_copy(b, own_columns).start()
        out_ref[b, :, own_columns] = state[:, pl.ds(aligned(start + core * shard, shard), shard)].T

    plane_begin(1)

    for m in range(4):
        for r in steps:
            line_copy(m, r).wait_send()
        for r in range(SIDE):
            sibling_copy(m, r, core).wait_send()

    def vec_drain(v):
        turn_copy(v).wait_send()
        for r in steps:
            for half in range(2):
                vec_copy(v, r, half).wait_send()

    vec_drain(0)

    @pl.when(helper)
    def _():
        vec_drain(1)
        for m in range(4):
            pass_on(m).wait_send()
        carry_copy(0).wait_send()

    vec_drain(2)
    for b in range(2):
        arrow_sibling_copy(b, core).wait_send()
        for r in steps:
            arrow_copy(b, r, arrow_mine[b]).wait_send()

    def drain(k, carry):
        for r in steps:
            copy_a(k, r).wait_send()
            copy_b(k, r).wait_send()

        @pl.when(x < SIDE - 1)
        def _():
            copy_next(k).wait_send()

        return carry

    lax.fori_loop(0, chunks, drain, 0)
    for b in range(2):
        out_copy(b, own_columns).wait_send()
        out_copy(b, other_columns).wait_recv()
        for h in range(2):
            for r in steps:
                line_copy_of(b, h, r).wait_send()
    loads[3].wait()
    loads[4].wait()

    for h in range(2):
        for copy in plane_targets(h):
            copy.wait_send()
            copy.wait_recv()
        for cross, owner in enumerate((core, other)):
            value = plane_heard[h, 1, 0] if cross else plane_sum[h]
            for r in steps:
                value = value + plane_heard[h, cross, r]
            columns = pl.ds(aligned(owner * lane + h * half_lane, half_lane), half_lane)
            tip_ref[:, columns] = jnp.dot(
                tip_inverse_ref[...],
                tip_right_ref[:, columns] - value,
                precision=lax.Precision.HIGHEST,
                preferred_element_type=jnp.float32,
            )


def body(right_sides, diag_inverse, coupling, carry_in, arrow_blocks, tip_right, tip_inverse):
    blocks, shard, columns = right_sides.shape
    effects = tip_right.shape[0]
    chip, span, lane = 2 * shard, 2 * shard * SIDE, columns // 2
    chunks = lane // CHUNK
    vmem = pl.BlockSpec(memory_space=pltpu.VMEM)
    hbm = pl.BlockSpec(memory_space=pl.ANY)
    half, full = jnp.bfloat16, jnp.float32
    dma = pltpu.SemaphoreType.DMA
    return pl.pallas_call(
        kernel,
        out_shape=(
            jax.ShapeDtypeStruct(right_sides.shape, half),
            jax.ShapeDtypeStruct(tip_right.shape, full),
        ),
        in_specs=[hbm] * 7,
        out_specs=(vmem, vmem),
        scratch_shapes=[
            pltpu.VMEM(right_sides.shape, half),
            pltpu.VMEM(carry_in.shape, half),
            pltpu.VMEM(arrow_blocks.shape, half),
            pltpu.VMEM(tip_right.shape, full),
            pltpu.VMEM(tip_inverse.shape, full),
            pltpu.VMEM((4, span, span), half),
            pltpu.VMEM((2, lane, span), half),
            pltpu.VMEM((lane, span), half),
            pltpu.VMEM((lane, span), full),
            pltpu.VMEM((lane, span), full),
            pltpu.VMEM((lane, span), half),
            pltpu.VMEM((lane, span), half),
            pltpu.VMEM((SIDE - 1, lane, span), half),
            pltpu.VMEM((SIDE - 1, lane, span), half),
            pltpu.VMEM((lane, span), half),
            pltpu.VMEM((lane, span), half),
            pltpu.VMEM((2, span, span), half),
            pltpu.VMEM((4, shard // 2, span), half),
            pltpu.VMEM((lane // 2, span), half),
            pltpu.VMEM((blocks, effects, span), half),
            pltpu.VMEM((3, lane, shard), half),
            pltpu.VMEM((blocks, shard, lane), half),
            pltpu.VMEM((2, 2, effects, lane // 2), full),
            pltpu.VMEM((2, 2, SIDE - 1, effects, lane // 2), full),
            pltpu.VMEM((2, effects, lane // 2), full),
            pltpu.VMEM((2, 2, SIDE, effects, lane // 2), full),
            dma((5,)), dma((4, SIDE)), dma((4, SIDE)), dma((4,)), dma((4, SIDE)), dma((4, SIDE)),
            dma((4,)), dma((4,)), dma((2,)), dma,
            dma((3,)), dma((3,)), dma((3, SIDE, 2)), dma((3, SIDE, 2)),
            dma((chunks, SIDE)), dma((chunks, SIDE)), dma((chunks, SIDE)), dma((chunks, SIDE)),
            dma((chunks,)), dma((chunks,)),
            dma((2,)), dma((2,)), dma((2, SIDE)), dma((2, SIDE)), dma((2,)),
            dma((2,)), dma((2,)), dma((2, 2, SIDE)), dma((2, 2, SIDE)), dma((2, 2, SIDE)), dma((2, 2, SIDE)),
        ],
        compiler_params=pltpu.CompilerParams(
            collective_id=0, has_side_effects=True, vmem_limit_bytes=VMEM_LIMIT
        ),
    )(right_sides, diag_inverse, coupling, carry_in, arrow_blocks, tip_right, tip_inverse)


def solution(mesh):
    placed = (
        P("tm", "mesh", None),
        P("tm", "mesh", None),
        P("tm", "mesh", None),
        P("mesh", None),
        P("tm", None, "mesh"),
        P(),
        P(),
    )
    return jax.shard_map(
        body, mesh=mesh, in_specs=placed, out_specs=(P("tm", "mesh", None), P()), check_vma=False
    )
```

```python
import functools

import jax
import jax.numpy as jnp
from jax import lax
from jax.experimental import pallas as pl
from jax.experimental.pallas import tpu as pltpu
from jax.sharding import PartitionSpec as P

MESH = pl.DeviceIdType.MESH
SIDE = 4
CHUNK = 16
VMEM_LIMIT = 63 << 20
AHEAD = 4


def device(x, y, z, core):
    return (lax.rem(x, SIDE), (lax.rem(y, SIDE) * SIDE + lax.rem(z, SIDE)) * 2 + core)


def times_transposed(rows, matrix):
    return lax.dot_general(
        rows, matrix, (((1,), (1,)), ((), ())), preferred_element_type=jnp.float32
    )


def kernel(
    rhs_hbm, diag_ref, coup_ref, carry_hbm, arrow_hbm, tip_right_hbm, tip_inverse_hbm,
    out_ref, tip_ref,
    rhs_ref, carry_ref, arrow_ref, tip_right_ref, tip_inverse_ref,
    mats, gathered, arriving, part_a, part_b, send_a, send_b, recv_a, recv_b,
    state_a, state_b, flipped, relay, relay_carry, arrow_line, turned, leaving, line_sum, line_heard, plane_sum, plane_heard,
    load_sem, mat_send, mat_recv, mat_local, sib_send, sib_recv,
    relay_recv, relay_send, carry_recv, carry_send,
    turn_send, turn_recv, vec_send, vec_recv,
    a_send, a_recv, b_send, b_recv, next_send, next_recv,
    arrow_sib_send, arrow_sib_recv, arrow_send, arrow_recv, arrow_local,
    out_send, out_recv, line_send, line_recv, plane_send, plane_recv,
):
    x = lax.axis_index("tm")
    place = lax.axis_index("mesh")
    y, z, core = place // (2 * SIDE), lax.rem(place // 2, SIDE), lax.rem(place, 2)
    other = 1 - core
    shard = rhs_ref.shape[1]
    chip = 2 * shard
    span = SIDE * chip
    lane = rhs_ref.shape[2] // 2
    chunks = lane // CHUNK
    effects = tip_ref.shape[0]
    sibling = device(x, y, z, other)
    along_z = lambda r: device(x, y, z + r, core)
    along_y = lambda r: device(x, y + r, z, core)
    along_x = lambda r: device(x + r, y, z, core)
    across_x = lambda r: device(x + r, y, z, other)
    steps = range(1, SIDE)

    loads = [
        pltpu.make_async_copy(src, dst, load_sem.at[i])
        for i, (src, dst) in enumerate((
            (rhs_hbm, rhs_ref), (carry_hbm, carry_ref), (arrow_hbm, arrow_ref),
            (tip_right_hbm, tip_right_ref), (tip_inverse_hbm, tip_inverse_ref),
        ))
    ]
    for load in loads:
        load.start()


    def aligned(value, unit):
        return pl.multiple_of(value, unit)

    def remote(src, dst, send, recv, target):
        return pltpu.make_async_remote_copy(
            src_ref=src, dst_ref=dst, send_sem=send, recv_sem=recv,
            device_id=target, device_id_type=MESH,
        )

    barrier = pltpu.get_barrier_semaphore()
    neighbours = [f(r) for f in (along_z, along_y, along_x, across_x) for r in steps]
    neighbours += [sibling]
    neighbours += [device(x + d, y + a, z + b, core) for d in (1, 3) for a, b in ((0, 2), (2, 0))]
    for target in neighbours:
        pl.semaphore_signal(barrier, inc=1, device_id=target, device_id_type=MESH)

    targets = (gathered.at[0], relay_carry, gathered.at[1])
    vec_lines = (along_y, along_y, along_z)
    vec_mine = (y, y, z)

    def slot(v, at, half):
        return targets[v].at[:, pl.ds(aligned(at * chip + half * shard, shard), shard)]

    def turn(v, value):
        value = value.T
        mine, theirs = value[:lane], value[lane:]
        mine, theirs = jnp.where(core == 0, mine, theirs), jnp.where(core == 0, theirs, mine)
        slot(v, vec_mine[v], core)[...] = mine
        turned[v] = theirs

    loads[0].wait()
    loads[1].wait()
    turn(0, rhs_ref[0])
    pl.when(x == 1)(lambda: turn(1, carry_ref[...]))
    turn(2, rhs_ref[1])
    pl.semaphore_wait(barrier, len(neighbours))

    sources = (diag_ref.at[0], coup_ref.at[0], diag_ref.at[1], coup_ref.at[1])
    lines = (along_z, along_z, along_y, along_y)
    mine = (z, z, y, y)

    def pieces(m, r):
        target_at = lax.rem(mine[m] + r, SIDE)
        rows = pl.ds(aligned(mine[m] * chip + core * shard, shard), shard)
        if m < 2:
            return [
                (
                    sources[m].at[:, pl.ds(aligned(a * span + target_at * chip, chip), chip)],
                    mats.at[m, rows, pl.ds(a * chip, chip)],
                )
                for a in range(SIDE)
            ]
        return [
            (
                sources[m].at[:, pl.ds(aligned(target_at * span, span), span)],
                mats.at[m, rows, :],
            )
        ]

    def send_near(m):
        for r in (1, 3):
            for src, dst in pieces(m, r):
                remote(src, dst, mat_send.at[m, r], mat_recv.at[m, r], lines[m](r)).start()

    def send_far(m):
        for src, dst in pieces(m, 2):
            remote(src, dst, mat_send.at[m, 2], mat_recv.at[m, 2], lines[m](2)).start()

    def send_round(m):
        rows = shard // 2
        found = pieces(m, 2)
        width = span // len(found)
        for n, (src, dst) in enumerate(found):
            columns = pl.ds(n * width, width)
            target = device(x + 3, y, z + 2, core) if m < 2 else device(x + 3, y + 2, z, core)
            remote(
                src.at[pl.ds(rows, rows)], relay.at[m, :, columns],
                mat_send.at[m, 2], relay_recv.at[m], target,
            ).start()
        start = aligned(mine[m] * chip + core * shard, shard)
        for n, (src, dst) in enumerate(found):
            columns = pl.ds(n * width, width)
            remote(
                src.at[pl.ds(0, rows)], mats.at[m, pl.ds(start, rows), columns],
                mat_send.at[m, 2], mat_recv.at[m, 2], lines[m](2),
            ).start()

    def pass_on(m):
        rows = shard // 2
        at = lax.rem(mine[m] + 2, SIDE)
        dst = mats.at[m, pl.ds(aligned(at * chip + core * shard + rows, rows), rows), :]
        return remote(relay.at[m], dst, relay_send.at[m], mat_recv.at[m, 2], device(0, y, z, core))

    def relay_wait(m):
        remote(relay.at[m], relay.at[m], relay_send.at[m], relay_recv.at[m], device(0, y, z, core)).wait_recv()

    def send_local(m):
        for src, dst in pieces(m, 0):
            remote(src, dst, sib_send.at[m, 0], sib_recv.at[m, 0], sibling).start()
            pltpu.make_async_copy(src, dst, mat_local.at[m]).start()

    def block(m, r, half):
        at = lax.rem(mine[m] - r + SIDE, SIDE)
        return mats.at[m, pl.ds(aligned(at * chip + half * shard, shard), shard), :]

    def line_copy(m, r):
        rows = block(m, r, core)
        return remote(rows, rows, mat_send.at[m, r], mat_recv.at[m, r], lines[m](r))

    def sibling_copy(m, r, half):
        rows = block(m, r, half)
        return remote(rows, rows, sib_send.at[m, r], sib_recv.at[m, r], sibling)

    def flip(m, r, half):
        if m % 2:
            at = lax.rem(mine[m] - r + SIDE, SIDE)
            columns = pl.ds(aligned(at * chip + half * shard, shard), shard)
            flipped[m // 2, :, columns] = block(m, r, half)[...].T

    def forward(m):
        for r in (1, 3, 2):
            line_copy(m, r).wait_recv()
            sibling_copy(m, r, core).start()
            flip(m, r, core)

    def complete(m):
        rows = block(m, 0, core)
        pltpu.make_async_copy(rows, rows, mat_local.at[m]).wait()
        flip(m, 0, core)
        for r in (0, 1, 3, 2):
            sibling_copy(m, r, other).wait_recv()
            flip(m, r, other)

    def turn_copy(v):
        return remote(
            turned.at[v], slot(v, vec_mine[v], core), turn_send.at[v], turn_recv.at[v], sibling
        )

    def vec_copy(v, r, half):
        rows = slot(v, vec_mine[v], half)
        return remote(
            rows, rows, vec_send.at[v, r, half], vec_recv.at[v, r, half], vec_lines[v](r)
        )

    def vec_begin(v):
        turn_copy(v).start()
        for r in (2, 1, 3):
            vec_copy(v, r, core).start()

    def vec_rest(v):
        rows = slot(v, vec_mine[v], other)
        remote(rows, rows, turn_send.at[v], turn_recv.at[v], sibling).wait_recv()
        for r in (2, 1, 3):
            vec_copy(v, r, other).start()

    def vec_wait(v):
        for r in (1, 3, 2):
            for half in range(2):
                rows = slot(v, lax.rem(vec_mine[v] - r + SIDE, SIDE), half)
                remote(
                    rows, rows, vec_send.at[v, r, half], vec_recv.at[v, r, half], vec_lines[v](r)
                ).wait_recv()

    arrow_lines = (along_z, along_y)
    arrow_mine = (z, y)

    def arrow_slot(b, at, half):
        return arrow_line.at[b, :, pl.ds(aligned(at * chip + half * shard, shard), shard)]

    def arrow_local_copy(b):
        return pltpu.make_async_copy(
            arrow_ref.at[b], arrow_slot(b, arrow_mine[b], core), arrow_local.at[b]
        )

    def arrow_sibling_copy(b, half):
        return remote(
            arrow_ref.at[b], arrow_slot(b, arrow_mine[b], half),
            arrow_sib_send.at[b], arrow_sib_recv.at[b], sibling,
        )

    def arrow_copy(b, r, at):
        rows = arrow_line.at[b, :, pl.ds(aligned(at * chip, chip), chip)]
        return remote(rows, rows, arrow_send.at[b, r], arrow_recv.at[b, r], arrow_lines[b](r))

    def carry_copy():
        return remote(relay_carry, arriving, carry_send, carry_recv, device(0, y, z, core))

    pl.when(x == 1)(lambda: vec_begin(1))
    vec_begin(0)

    @pl.when(x == 0)
    def _():
        for m in range(2):
            send_round(m)

    @pl.when(x < 3)
    def _():
        for m in range(2):
            send_near(m)

    turn_copy(2).start()
    pl.when(x == 1)(lambda: vec_rest(1))
    vec_rest(0)

    @pl.when(x == 0)
    def _():
        for m in range(2, 4):
            send_round(m)

    @pl.when(x < 3)
    def _():
        for m in range(2, 4):
            send_near(m)

    @pl.when(jnp.logical_or(x == 1, x == 2))
    def _():
        for m in range(4):
            send_far(m)

    for m in range(4):
        send_local(m)

    @pl.when(x == 1)
    def _():
        vec_wait(1)
        carry_copy().start()

    @pl.when(x == 3)
    def _():
        for m in (0, 1):
            relay_wait(m)
            pass_on(m).start()
        for m in (2, 3):
            relay_wait(m)
            pass_on(m).start()
        for m in range(4):
            send_near(m)
        for m in range(4):
            send_far(m)

    loads[2].wait()
    for b in range(2):
        arrow_local_copy(b).start()
        arrow_sibling_copy(b, core).start()

    forward(0)
    for r in (2, 1, 3):
        vec_copy(2, r, core).start()
    vec_rest(2)
    vec_wait(0)
    complete(0)
    part_a[...] = times_transposed(gathered[0], mats[0])
    forward(1)
    complete(1)

    @pl.when(x == 0)
    def _():
        carry_copy().wait_recv()

    def rows_of(k):
        return pl.ds(aligned(k * CHUNK, CHUNK), CHUNK)

    def chunk_copy(src, dst, send, recv, line, k, r):
        return remote(
            src.at[rows_of(k)], dst.at[r - 1, rows_of(k)], send.at[k, r], recv.at[k, r], line(r)
        )

    copy_a = functools.partial(chunk_copy, send_a, recv_a, a_send, a_recv, along_z)
    copy_b = functools.partial(chunk_copy, send_b, recv_b, b_send, b_recv, along_y)

    def copy_next(k):
        return remote(
            state_b.at[rows_of(k)], arriving.at[rows_of(k)], next_send.at[k], next_recv.at[k], along_x(1)
        )

    def spread(terms, sent, matrix, source, copy, k):
        rows = rows_of(k)
        value = terms[rows, :] - jnp.dot(
            source[rows, :], matrix[...], preferred_element_type=jnp.float32
        )
        terms[rows, :] = value
        sent[rows, :] = value.astype(jnp.bfloat16)
        for r in (2, 1, 3):
            copy(k, r).start()

    def settle(terms, received, state, copy, k):
        rows = rows_of(k)
        for r in (1, 3, 2):
            copy(k, r).wait_recv()
        value = terms[rows, :]
        for r in steps:
            value = value + received[r - 1, rows, :].astype(jnp.float32)
        state[rows, :] = value.astype(jnp.bfloat16)

    def first(k):
        @pl.when(x > 0)
        def _():
            copy_next(k).wait_recv()

        spread(part_a, send_a, flipped.at[0], arriving, copy_a, k)

    def second(k):
        settle(part_a, recv_a, state_a, copy_a, k)
        spread(part_b, send_b, flipped.at[1], state_a, copy_b, k)

    def third(k):
        settle(part_b, recv_b, state_b, copy_b, k)

        @pl.when(x < SIDE - 1)
        def _():
            copy_next(k).start()

    def second_block():
        forward(2)
        forward(3)
        vec_wait(2)
        complete(2)
        part_b[...] = times_transposed(gathered[1], mats[2])
        complete(3)
        for b in range(2):
            arrow_sibling_copy(b, other).wait_recv()
            arrow_local_copy(b).wait()
            for r in steps:
                arrow_copy(b, r, arrow_mine[b]).start()

    pl.when(x > 0)(second_block)

    def lead(k, carry):
        first(k)
        return carry

    lax.fori_loop(0, AHEAD, lead, 0)
    pl.when(x == 0)(second_block)

    def step(n, carry):
        @pl.when(n >= 2 * AHEAD)
        def _():
            third(n - 2 * AHEAD)

        @pl.when(jnp.logical_and(n >= AHEAD, n < chunks + AHEAD))
        def _():
            second(n - AHEAD)

        @pl.when(n < chunks)
        def _():
            first(n)

        return carry

    sum_lines = (along_y, along_z)
    half_lane = lane // 2

    def line_copy_of(b, h, r):
        return remote(
            line_sum.at[b, h], line_heard.at[b, h, r - 1],
            line_send.at[b, h, r], line_recv.at[b, h, r], sum_lines[b](r),
        )

    def line_begin(b, h):
        state = (state_a, state_b)[b]
        line_sum[b, h] = times_transposed(
            arrow_line[b], state[pl.ds(h * half_lane, half_lane), :]
        )
        for r in (2, 1, 3):
            line_copy_of(b, h, r).start()

    def plane_targets(h):
        found = []
        for r in range(SIDE):
            if r:
                found.append((0, r, along_x(r)))
            found.append((1, r, across_x(r) if r else sibling))
        return [
            remote(
                plane_sum.at[h], plane_heard.at[h, cross, r],
                plane_send.at[h, cross, r], plane_recv.at[h, cross, r], target,
            )
            for cross, r, target in found
        ]

    def plane_begin(h):
        value = jnp.zeros((effects, half_lane), jnp.float32)
        for b in range(2):
            value = value + line_sum[b, h]
            for r in steps:
                line_copy_of(b, h, r).wait_recv()
                value = value + line_heard[b, h, r - 1]
        plane_sum[h] = value
        for copy in plane_targets(h):
            copy.start()

    middle = chunks // 2 + 2 * AHEAD
    lax.fori_loop(AHEAD, middle, step, 0)
    for b in range(2):
        for r in steps:
            arrow_copy(b, r, lax.rem(arrow_mine[b] - r + SIDE, SIDE)).wait_recv()
    line_begin(0, 0)
    line_begin(1, 0)
    lax.fori_loop(middle, chunks + 2 * AHEAD, step, 0)
    line_begin(1, 1)
    line_begin(0, 1)
    plane_begin(0)

    def out_copy(b, columns):
        return remote(
            leaving.at[b], out_ref.at[b, :, columns], out_send.at[b], out_recv.at[b], sibling
        )

    own_columns = pl.ds(aligned(core * lane, lane), lane)
    other_columns = pl.ds(aligned(other * lane, lane), lane)
    for b, (state, at) in enumerate([(state_a, z), (state_b, y)]):
        start = at * chip
        leaving[b] = state[:, pl.ds(aligned(start + other * shard, shard), shard)].T
        out_copy(b, own_columns).start()
        out_ref[b, :, own_columns] = state[:, pl.ds(aligned(start + core * shard, shard), shard)].T

    plane_begin(1)

    for m in range(4):
        for r in steps:
            line_copy(m, r).wait_send()
        for r in range(SIDE):
            sibling_copy(m, r, core).wait_send()

    def vec_drain(v):
        turn_copy(v).wait_send()
        for r in steps:
            for half in range(2):
                vec_copy(v, r, half).wait_send()

    vec_drain(0)

    @pl.when(x == 1)
    def _():
        vec_drain(1)
        carry_copy().wait_send()

    @pl.when(x == 3)
    def _():
        for m in range(4):
            pass_on(m).wait_send()

    vec_drain(2)
    for b in range(2):
        arrow_sibling_copy(b, core).wait_send()
        for r in steps:
            arrow_copy(b, r, arrow_mine[b]).wait_send()

    def drain(k, carry):
        for r in steps:
            copy_a(k, r).wait_send()
            copy_b(k, r).wait_send()

        @pl.when(x < SIDE - 1)
        def _():
            copy_next(k).wait_send()

        return carry

    lax.fori_loop(0, chunks, drain, 0)
    for b in range(2):
        out_copy(b, own_columns).wait_send()
        out_copy(b, other_columns).wait_recv()
        for h in range(2):
            for r in steps:
                line_copy_of(b, h, r).wait_send()
    loads[3].wait()
    loads[4].wait()

    for h in range(2):
        for copy in plane_targets(h):
            copy.wait_send()
            copy.wait_recv()
        for cross, owner in enumerate((core, other)):
            value = plane_heard[h, 1, 0] if cross else plane_sum[h]
            for r in steps:
                value = value + plane_heard[h, cross, r]
            columns = pl.ds(aligned(owner * lane + h * half_lane, half_lane), half_lane)
            tip_ref[:, columns] = jnp.dot(
                tip_inverse_ref[...],
                tip_right_ref[:, columns] - value,
                precision=lax.Precision.HIGHEST,
                preferred_element_type=jnp.float32,
            )


def body(right_sides, diag_inverse, coupling, carry_in, arrow_blocks, tip_right, tip_inverse):
    blocks, shard, columns = right_sides.shape
    effects = tip_right.shape[0]
    chip, span, lane = 2 * shard, 2 * shard * SIDE, columns // 2
    chunks = lane // CHUNK
    vmem = pl.BlockSpec(memory_space=pltpu.VMEM)
    hbm = pl.BlockSpec(memory_space=pl.ANY)
    half, full = jnp.bfloat16, jnp.float32
    dma = pltpu.SemaphoreType.DMA
    return pl.pallas_call(
        kernel,
        out_shape=(
            jax.ShapeDtypeStruct(right_sides.shape, half),
            jax.ShapeDtypeStruct(tip_right.shape, full),
        ),
        in_specs=[hbm] * 7,
        out_specs=(vmem, vmem),
        scratch_shapes=[
            pltpu.VMEM(right_sides.shape, half),
            pltpu.VMEM(carry_in.shape, half),
            pltpu.VMEM(arrow_blocks.shape, half),
            pltpu.VMEM(tip_right.shape, full),
            pltpu.VMEM(tip_inverse.shape, full),
            pltpu.VMEM((4, span, span), half),
            pltpu.VMEM((2, lane, span), half),
            pltpu.VMEM((lane, span), half),
            pltpu.VMEM((lane, span), full),
            pltpu.VMEM((lane, span), full),
            pltpu.VMEM((lane, span), half),
            pltpu.VMEM((lane, span), half),
            pltpu.VMEM((SIDE - 1, lane, span), half),
            pltpu.VMEM((SIDE - 1, lane, span), half),
            pltpu.VMEM((lane, span), half),
            pltpu.VMEM((lane, span), half),
            pltpu.VMEM((2, span, span), half),
            pltpu.VMEM((4, shard // 2, span), half),
            pltpu.VMEM((lane, span), half),
            pltpu.VMEM((blocks, effects, span), half),
            pltpu.VMEM((3, lane, shard), half),
            pltpu.VMEM((blocks, shard, lane), half),
            pltpu.VMEM((2, 2, effects, lane // 2), full),
            pltpu.VMEM((2, 2, SIDE - 1, effects, lane // 2), full),
            pltpu.VMEM((2, effects, lane // 2), full),
            pltpu.VMEM((2, 2, SIDE, effects, lane // 2), full),
            dma((5,)), dma((4, SIDE)), dma((4, SIDE)), dma((4,)), dma((4, SIDE)), dma((4, SIDE)),
            dma((4,)), dma((4,)), dma, dma,
            dma((3,)), dma((3,)), dma((3, SIDE, 2)), dma((3, SIDE, 2)),
            dma((chunks, SIDE)), dma((chunks, SIDE)), dma((chunks, SIDE)), dma((chunks, SIDE)),
            dma((chunks,)), dma((chunks,)),
            dma((2,)), dma((2,)), dma((2, SIDE)), dma((2, SIDE)), dma((2,)),
            dma((2,)), dma((2,)), dma((2, 2, SIDE)), dma((2, 2, SIDE)), dma((2, 2, SIDE)), dma((2, 2, SIDE)),
        ],
        compiler_params=pltpu.CompilerParams(
            collective_id=0, has_side_effects=True, vmem_limit_bytes=VMEM_LIMIT
        ),
    )(right_sides, diag_inverse, coupling, carry_in, arrow_blocks, tip_right, tip_inverse)


def solution(mesh):
    placed = (
        P("tm", "mesh", None),
        P("tm", "mesh", None),
        P("tm", "mesh", None),
        P("mesh", None),
        P("tm", None, "mesh"),
        P(),
        P(),
    )
    return jax.shard_map(
        body, mesh=mesh, in_specs=placed, out_specs=(P("tm", "mesh", None), P()), check_vma=False
    )
```

```python
import functools

import jax
import jax.numpy as jnp
from jax import lax
from jax.experimental import pallas as pl
from jax.experimental.pallas import tpu as pltpu
from jax.sharding import PartitionSpec as P

MESH = pl.DeviceIdType.MESH
SIDE = 4
CHUNK = 16
VMEM_LIMIT = 63 << 20
AHEAD = 4


def device(x, y, z, core):
    return (lax.rem(x, SIDE), (lax.rem(y, SIDE) * SIDE + lax.rem(z, SIDE)) * 2 + core)


def times_transposed(rows, matrix):
    return lax.dot_general(
        rows, matrix, (((1,), (1,)), ((), ())), preferred_element_type=jnp.float32
    )


def kernel(
    rhs_hbm, diag_ref, coup_ref, carry_hbm, arrow_hbm, tip_right_hbm, tip_inverse_hbm,
    out_ref, tip_ref,
    rhs_ref, carry_ref, arrow_ref, tip_right_ref, tip_inverse_ref,
    mats, gathered, arriving, part_a, part_b, send_a, send_b, recv_a, recv_b,
    state_a, state_b, flipped, relay, relay_carry, arrow_line, turned, leaving, line_sum, line_heard, plane_sum, plane_heard,
    load_sem, mat_send, mat_recv, mat_local, sib_send, sib_recv,
    relay_recv, relay_send, carry_recv, carry_send,
    turn_send, turn_recv, vec_send, vec_recv,
    a_send, a_recv, b_send, b_recv, next_send, next_recv,
    arrow_sib_send, arrow_sib_recv, arrow_send, arrow_recv, arrow_local,
    out_send, out_recv, line_send, line_recv, plane_send, plane_recv,
):
    x = lax.axis_index("tm")
    place = lax.axis_index("mesh")
    y, z, core = place // (2 * SIDE), lax.rem(place // 2, SIDE), lax.rem(place, 2)
    other = 1 - core
    shard = rhs_ref.shape[1]
    chip = 2 * shard
    span = SIDE * chip
    lane = rhs_ref.shape[2] // 2
    chunks = lane // CHUNK
    effects = tip_ref.shape[0]
    sibling = device(x, y, z, other)
    along_z = lambda r: device(x, y, z + r, core)
    along_y = lambda r: device(x, y + r, z, core)
    along_x = lambda r: device(x + r, y, z, core)
    across_x = lambda r: device(x + r, y, z, other)
    steps = range(1, SIDE)

    loads = [
        pltpu.make_async_copy(src, dst, load_sem.at[i])
        for i, (src, dst) in enumerate((
            (rhs_hbm, rhs_ref), (carry_hbm, carry_ref), (arrow_hbm, arrow_ref),
            (tip_right_hbm, tip_right_ref), (tip_inverse_hbm, tip_inverse_ref),
        ))
    ]
    for load in loads:
        load.start()


    def aligned(value, unit):
        return pl.multiple_of(value, unit)

    def remote(src, dst, send, recv, target):
        return pltpu.make_async_remote_copy(
            src_ref=src, dst_ref=dst, send_sem=send, recv_sem=recv,
            device_id=target, device_id_type=MESH,
        )

    barrier = pltpu.get_barrier_semaphore()
    neighbours = [f(r) for f in (along_z, along_y, along_x, across_x) for r in steps]
    neighbours += [sibling]
    neighbours += [device(x + d, y + a, z + b, core) for d in (1, 3) for a, b in ((0, 2), (2, 0))]
    for target in neighbours:
        pl.semaphore_signal(barrier, inc=1, device_id=target, device_id_type=MESH)

    targets = (gathered.at[0], relay_carry, gathered.at[1])
    vec_lines = (along_y, along_y, along_z)
    vec_mine = (y, y, z)

    def slot(v, at, half):
        return targets[v].at[:, pl.ds(aligned(at * chip + half * shard, shard), shard)]

    def turn(v, value):
        value = value.T
        mine, theirs = value[:lane], value[lane:]
        mine, theirs = jnp.where(core == 0, mine, theirs), jnp.where(core == 0, theirs, mine)
        slot(v, vec_mine[v], core)[...] = mine
        turned[v] = theirs

    loads[0].wait()
    loads[1].wait()
    turn(0, rhs_ref[0])
    pl.when(x == 1)(lambda: turn(1, carry_ref[...]))
    turn(2, rhs_ref[1])
    pl.semaphore_wait(barrier, len(neighbours))

    sources = (diag_ref.at[0], coup_ref.at[0], diag_ref.at[1], coup_ref.at[1])
    lines = (along_z, along_z, along_y, along_y)
    mine = (z, z, y, y)

    def pieces(m, r):
        target_at = lax.rem(mine[m] + r, SIDE)
        rows = pl.ds(aligned(mine[m] * chip + core * shard, shard), shard)
        if m < 2:
            return [
                (
                    sources[m].at[:, pl.ds(aligned(a * span + target_at * chip, chip), chip)],
                    mats.at[m, rows, pl.ds(a * chip, chip)],
                )
                for a in range(SIDE)
            ]
        return [
            (
                sources[m].at[:, pl.ds(aligned(target_at * span, span), span)],
                mats.at[m, rows, :],
            )
        ]

    def send_near(m):
        for r in (1, 3):
            for src, dst in pieces(m, r):
                remote(src, dst, mat_send.at[m, r], mat_recv.at[m, r], lines[m](r)).start()

    def send_far(m):
        for src, dst in pieces(m, 2):
            remote(src, dst, mat_send.at[m, 2], mat_recv.at[m, 2], lines[m](2)).start()

    def send_round(m):
        rows = shard - (96, 80)[m // 2]
        found = pieces(m, 2)
        width = span // len(found)
        for n, (src, dst) in enumerate(found):
            columns = pl.ds(n * width, width)
            target = device(x + 3, y, z + 2, core) if m < 2 else device(x + 3, y + 2, z, core)
            remote(
                src.at[pl.ds(rows, shard - rows)], relay.at[m, pl.ds(0, shard - rows), columns],
                mat_send.at[m, 2], relay_recv.at[m], target,
            ).start()
        start = aligned(mine[m] * chip + core * shard, shard)
        for n, (src, dst) in enumerate(found):
            columns = pl.ds(n * width, width)
            remote(
                src.at[pl.ds(0, rows)], mats.at[m, pl.ds(start, rows), columns],
                mat_send.at[m, 2], mat_recv.at[m, 2], lines[m](2),
            ).start()

    def pass_on(m):
        rows = (96, 80)[m // 2]
        at = lax.rem(mine[m] + 2, SIDE) * chip + core * shard + shard - rows
        dst = mats.at[m, pl.ds(aligned(at, 16), rows), :]
        return remote(
            relay.at[m, pl.ds(0, rows)], dst, relay_send.at[m], mat_recv.at[m, 2], device(0, y, z, core)
        )

    def relay_wait(m):
        held = relay.at[m, pl.ds(0, (96, 80)[m // 2])]
        remote(held, held, relay_send.at[m], relay_recv.at[m], device(0, y, z, core)).wait_recv()

    def send_local(m):
        for src, dst in pieces(m, 0):
            remote(src, dst, sib_send.at[m, 0], sib_recv.at[m, 0], sibling).start()
            pltpu.make_async_copy(src, dst, mat_local.at[m]).start()

    def block(m, r, half):
        at = lax.rem(mine[m] - r + SIDE, SIDE)
        return mats.at[m, pl.ds(aligned(at * chip + half * shard, shard), shard), :]

    def line_copy(m, r):
        rows = block(m, r, core)
        return remote(rows, rows, mat_send.at[m, r], mat_recv.at[m, r], lines[m](r))

    def sibling_copy(m, r, half):
        rows = block(m, r, half)
        return remote(rows, rows, sib_send.at[m, r], sib_recv.at[m, r], sibling)

    def flip(m, r, half):
        if m % 2:
            at = lax.rem(mine[m] - r + SIDE, SIDE)
            columns = pl.ds(aligned(at * chip + half * shard, shard), shard)
            flipped[m // 2, :, columns] = block(m, r, half)[...].T

    def forward(m):
        for r in (1, 3, 2):
            line_copy(m, r).wait_recv()
            sibling_copy(m, r, core).start()
            flip(m, r, core)

    def complete(m):
        rows = block(m, 0, core)
        pltpu.make_async_copy(rows, rows, mat_local.at[m]).wait()
        flip(m, 0, core)
        for r in (0, 1, 3, 2):
            sibling_copy(m, r, other).wait_recv()
            flip(m, r, other)

    def turn_copy(v):
        return remote(
            turned.at[v], slot(v, vec_mine[v], core), turn_send.at[v], turn_recv.at[v], sibling
        )

    def vec_copy(v, r, half):
        rows = slot(v, vec_mine[v], half)
        return remote(
            rows, rows, vec_send.at[v, r, half], vec_recv.at[v, r, half], vec_lines[v](r)
        )

    def vec_begin(v):
        turn_copy(v).start()
        for r in (2, 1, 3):
            vec_copy(v, r, core).start()

    def vec_rest(v):
        rows = slot(v, vec_mine[v], other)
        remote(rows, rows, turn_send.at[v], turn_recv.at[v], sibling).wait_recv()
        for r in (2, 1, 3):
            vec_copy(v, r, other).start()

    def vec_wait(v):
        for r in (1, 3, 2):
            for half in range(2):
                rows = slot(v, lax.rem(vec_mine[v] - r + SIDE, SIDE), half)
                remote(
                    rows, rows, vec_send.at[v, r, half], vec_recv.at[v, r, half], vec_lines[v](r)
                ).wait_recv()

    arrow_lines = (along_z, along_y)
    arrow_mine = (z, y)

    def arrow_slot(b, at, half):
        return arrow_line.at[b, :, pl.ds(aligned(at * chip + half * shard, shard), shard)]

    def arrow_local_copy(b):
        return pltpu.make_async_copy(
            arrow_ref.at[b], arrow_slot(b, arrow_mine[b], core), arrow_local.at[b]
        )

    def arrow_sibling_copy(b, half):
        return remote(
            arrow_ref.at[b], arrow_slot(b, arrow_mine[b], half),
            arrow_sib_send.at[b], arrow_sib_recv.at[b], sibling,
        )

    def arrow_copy(b, r, at):
        rows = arrow_line.at[b, :, pl.ds(aligned(at * chip, chip), chip)]
        return remote(rows, rows, arrow_send.at[b, r], arrow_recv.at[b, r], arrow_lines[b](r))

    def carry_copy():
        return remote(relay_carry, arriving, carry_send, carry_recv, device(0, y, z, core))

    pl.when(x == 1)(lambda: vec_begin(1))
    vec_begin(0)

    @pl.when(x == 0)
    def _():
        for m in range(2):
            send_round(m)

    @pl.when(x < 3)
    def _():
        for m in range(2):
            send_near(m)

    turn_copy(2).start()
    pl.when(x == 1)(lambda: vec_rest(1))
    vec_rest(0)

    @pl.when(x == 0)
    def _():
        for m in range(2, 4):
            send_round(m)

    @pl.when(x < 3)
    def _():
        for m in range(2, 4):
            send_near(m)

    @pl.when(jnp.logical_or(x == 1, x == 2))
    def _():
        for m in range(4):
            send_far(m)

    for m in range(4):
        send_local(m)

    @pl.when(x == 1)
    def _():
        vec_wait(1)
        carry_copy().start()

    @pl.when(x == 3)
    def _():
        for m in (0, 1):
            relay_wait(m)
            pass_on(m).start()
        for m in (2, 3):
            relay_wait(m)
            pass_on(m).start()
        for m in range(4):
            send_near(m)
        for m in range(4):
            send_far(m)

    loads[2].wait()
    for b in range(2):
        arrow_local_copy(b).start()
        arrow_sibling_copy(b, core).start()

    forward(0)
    for r in (2, 1, 3):
        vec_copy(2, r, core).start()
    vec_rest(2)
    vec_wait(0)
    complete(0)
    part_a[...] = times_transposed(gathered[0], mats[0])
    forward(1)
    complete(1)

    @pl.when(x == 0)
    def _():
        carry_copy().wait_recv()

    def rows_of(k):
        return pl.ds(aligned(k * CHUNK, CHUNK), CHUNK)

    def chunk_copy(src, dst, send, recv, line, k, r):
        return remote(
            src.at[rows_of(k)], dst.at[r - 1, rows_of(k)], send.at[k, r], recv.at[k, r], line(r)
        )

    copy_a = functools.partial(chunk_copy, send_a, recv_a, a_send, a_recv, along_z)
    copy_b = functools.partial(chunk_copy, send_b, recv_b, b_send, b_recv, along_y)

    def copy_next(k):
        return remote(
            state_b.at[rows_of(k)], arriving.at[rows_of(k)], next_send.at[k], next_recv.at[k], along_x(1)
        )

    def spread(terms, sent, matrix, source, copy, k):
        rows = rows_of(k)
        value = terms[rows, :] - jnp.dot(
            source[rows, :], matrix[...], preferred_element_type=jnp.float32
        )
        terms[rows, :] = value
        sent[rows, :] = value.astype(jnp.bfloat16)
        for r in (2, 1, 3):
            copy(k, r).start()

    def settle(terms, received, state, copy, k):
        rows = rows_of(k)
        for r in (1, 3, 2):
            copy(k, r).wait_recv()
        value = terms[rows, :]
        for r in steps:
            value = value + received[r - 1, rows, :].astype(jnp.float32)
        state[rows, :] = value.astype(jnp.bfloat16)

    def first(k):
        @pl.when(x > 0)
        def _():
            copy_next(k).wait_recv()

        spread(part_a, send_a, flipped.at[0], arriving, copy_a, k)

    def second(k):
        settle(part_a, recv_a, state_a, copy_a, k)
        spread(part_b, send_b, flipped.at[1], state_a, copy_b, k)

    def third(k):
        settle(part_b, recv_b, state_b, copy_b, k)

        @pl.when(x < SIDE - 1)
        def _():
            copy_next(k).start()

    def second_block():
        forward(2)
        forward(3)
        vec_wait(2)
        complete(2)
        part_b[...] = times_transposed(gathered[1], mats[2])
        complete(3)
        for b in range(2):
            arrow_sibling_copy(b, other).wait_recv()
            arrow_local_copy(b).wait()
            for r in steps:
                arrow_copy(b, r, arrow_mine[b]).start()

    pl.when(x > 0)(second_block)

    def lead(k, carry):
        first(k)
        return carry

    lax.fori_loop(0, AHEAD, lead, 0)
    pl.when(x == 0)(second_block)

    def step(n, carry):
        @pl.when(n >= 2 * AHEAD)
        def _():
            third(n - 2 * AHEAD)

        @pl.when(jnp.logical_and(n >= AHEAD, n < chunks + AHEAD))
        def _():
            second(n - AHEAD)

        @pl.when(n < chunks)
        def _():
            first(n)

        return carry

    sum_lines = (along_y, along_z)
    half_lane = lane // 2

    def line_copy_of(b, h, r):
        return remote(
            line_sum.at[b, h], line_heard.at[b, h, r - 1],
            line_send.at[b, h, r], line_recv.at[b, h, r], sum_lines[b](r),
        )

    def line_begin(b, h):
        state = (state_a, state_b)[b]
        line_sum[b, h] = times_transposed(
            arrow_line[b], state[pl.ds(h * half_lane, half_lane), :]
        )
        for r in (2, 1, 3):
            line_copy_of(b, h, r).start()

    def plane_targets(h):
        found = []
        for r in range(SIDE):
            if r:
                found.append((0, r, along_x(r)))
            found.append((1, r, across_x(r) if r else sibling))
        return [
            remote(
                plane_sum.at[h], plane_heard.at[h, cross, r],
                plane_send.at[h, cross, r], plane_recv.at[h, cross, r], target,
            )
            for cross, r, target in found
        ]

    def plane_begin(h):
        value = jnp.zeros((effects, half_lane), jnp.float32)
        for b in range(2):
            value = value + line_sum[b, h]
            for r in steps:
                line_copy_of(b, h, r).wait_recv()
                value = value + line_heard[b, h, r - 1]
        plane_sum[h] = value
        for copy in plane_targets(h):
            copy.start()

    middle = chunks // 2 + 2 * AHEAD
    lax.fori_loop(AHEAD, middle, step, 0)
    for b in range(2):
        for r in steps:
            arrow_copy(b, r, lax.rem(arrow_mine[b] - r + SIDE, SIDE)).wait_recv()
    line_begin(0, 0)
    line_begin(1, 0)
    lax.fori_loop(middle, chunks + 2 * AHEAD, step, 0)
    line_begin(1, 1)
    line_begin(0, 1)
    plane_begin(0)

    def out_copy(b, columns):
        return remote(
            leaving.at[b], out_ref.at[b, :, columns], out_send.at[b], out_recv.at[b], sibling
        )

    own_columns = pl.ds(aligned(core * lane, lane), lane)
    other_columns = pl.ds(aligned(other * lane, lane), lane)
    for b, (state, at) in enumerate([(state_a, z), (state_b, y)]):
        start = at * chip
        leaving[b] = state[:, pl.ds(aligned(start + other * shard, shard), shard)].T
        out_copy(b, own_columns).start()
        out_ref[b, :, own_columns] = state[:, pl.ds(aligned(start + core * shard, shard), shard)].T

    plane_begin(1)

    for m in range(4):
        for r in steps:
            line_copy(m, r).wait_send()
        for r in range(SIDE):
            sibling_copy(m, r, core).wait_send()

    def vec_drain(v):
        turn_copy(v).wait_send()
        for r in steps:
            for half in range(2):
                vec_copy(v, r, half).wait_send()

    vec_drain(0)

    @pl.when(x == 1)
    def _():
        vec_drain(1)
        carry_copy().wait_send()

    @pl.when(x == 3)
    def _():
        for m in range(4):
            pass_on(m).wait_send()

    vec_drain(2)
    for b in range(2):
        arrow_sibling_copy(b, core).wait_send()
        for r in steps:
            arrow_copy(b, r, arrow_mine[b]).wait_send()

    def drain(k, carry):
        for r in steps:
            copy_a(k, r).wait_send()
            copy_b(k, r).wait_send()

        @pl.when(x < SIDE - 1)
        def _():
            copy_next(k).wait_send()

        return carry

    lax.fori_loop(0, chunks, drain, 0)
    for b in range(2):
        out_copy(b, own_columns).wait_send()
        out_copy(b, other_columns).wait_recv()
        for h in range(2):
            for r in steps:
                line_copy_of(b, h, r).wait_send()
    loads[3].wait()
    loads[4].wait()

    for h in range(2):
        for copy in plane_targets(h):
            copy.wait_send()
            copy.wait_recv()
        for cross, owner in enumerate((core, other)):
            value = plane_heard[h, 1, 0] if cross else plane_sum[h]
            for r in steps:
                value = value + plane_heard[h, cross, r]
            columns = pl.ds(aligned(owner * lane + h * half_lane, half_lane), half_lane)
            tip_ref[:, columns] = jnp.dot(
                tip_inverse_ref[...],
                tip_right_ref[:, columns] - value,
                precision=lax.Precision.HIGHEST,
                preferred_element_type=jnp.float32,
            )


def body(right_sides, diag_inverse, coupling, carry_in, arrow_blocks, tip_right, tip_inverse):
    blocks, shard, columns = right_sides.shape
    effects = tip_right.shape[0]
    chip, span, lane = 2 * shard, 2 * shard * SIDE, columns // 2
    chunks = lane // CHUNK
    vmem = pl.BlockSpec(memory_space=pltpu.VMEM)
    hbm = pl.BlockSpec(memory_space=pl.ANY)
    half, full = jnp.bfloat16, jnp.float32
    dma = pltpu.SemaphoreType.DMA
    return pl.pallas_call(
        kernel,
        out_shape=(
            jax.ShapeDtypeStruct(right_sides.shape, half),
            jax.ShapeDtypeStruct(tip_right.shape, full),
        ),
        in_specs=[hbm] * 7,
        out_specs=(vmem, vmem),
        scratch_shapes=[
            pltpu.VMEM(right_sides.shape, half),
            pltpu.VMEM(carry_in.shape, half),
            pltpu.VMEM(arrow_blocks.shape, half),
            pltpu.VMEM(tip_right.shape, full),
            pltpu.VMEM(tip_inverse.shape, full),
            pltpu.VMEM((4, span, span), half),
            pltpu.VMEM((2, lane, span), half),
            pltpu.VMEM((lane, span), half),
            pltpu.VMEM((lane, span), full),
            pltpu.VMEM((lane, span), full),
            pltpu.VMEM((lane, span), half),
            pltpu.VMEM((lane, span), half),
            pltpu.VMEM((SIDE - 1, lane, span), half),
            pltpu.VMEM((SIDE - 1, lane, span), half),
            pltpu.VMEM((lane, span), half),
            pltpu.VMEM((lane, span), half),
            pltpu.VMEM((2, span, span), half),
            pltpu.VMEM((4, shard, span), half),
            pltpu.VMEM((lane, span), half),
            pltpu.VMEM((blocks, effects, span), half),
            pltpu.VMEM((3, lane, shard), half),
            pltpu.VMEM((blocks, shard, lane), half),
            pltpu.VMEM((2, 2, effects, lane // 2), full),
            pltpu.VMEM((2, 2, SIDE - 1, effects, lane // 2), full),
            pltpu.VMEM((2, effects, lane // 2), full),
            pltpu.VMEM((2, 2, SIDE, effects, lane // 2), full),
            dma((5,)), dma((4, SIDE)), dma((4, SIDE)), dma((4,)), dma((4, SIDE)), dma((4, SIDE)),
            dma((4,)), dma((4,)), dma, dma,
            dma((3,)), dma((3,)), dma((3, SIDE, 2)), dma((3, SIDE, 2)),
            dma((chunks, SIDE)), dma((chunks, SIDE)), dma((chunks, SIDE)), dma((chunks, SIDE)),
            dma((chunks,)), dma((chunks,)),
            dma((2,)), dma((2,)), dma((2, SIDE)), dma((2, SIDE)), dma((2,)),
            dma((2,)), dma((2,)), dma((2, 2, SIDE)), dma((2, 2, SIDE)), dma((2, 2, SIDE)), dma((2, 2, SIDE)),
        ],
        compiler_params=pltpu.CompilerParams(
            collective_id=0, has_side_effects=True, vmem_limit_bytes=VMEM_LIMIT
        ),
    )(right_sides, diag_inverse, coupling, carry_in, arrow_blocks, tip_right, tip_inverse)


def solution(mesh):
    placed = (
        P("tm", "mesh", None),
        P("tm", "mesh", None),
        P("tm", "mesh", None),
        P("mesh", None),
        P("tm", None, "mesh"),
        P(),
        P(),
    )
    return jax.shard_map(
        body, mesh=mesh, in_specs=placed, out_specs=(P("tm", "mesh", None), P()), check_vma=False
    )
```

```python
import functools

import jax
import jax.numpy as jnp
from jax import lax
from jax.experimental import pallas as pl
from jax.experimental.pallas import tpu as pltpu
from jax.sharding import PartitionSpec as P

MESH = pl.DeviceIdType.MESH
SIDE = 4
CHUNK = 16
VMEM_LIMIT = 63 << 20
AHEAD = 4


def device(x, y, z, core):
    return (lax.rem(x, SIDE), (lax.rem(y, SIDE) * SIDE + lax.rem(z, SIDE)) * 2 + core)


def times_transposed(rows, matrix):
    return lax.dot_general(
        rows, matrix, (((1,), (1,)), ((), ())), preferred_element_type=jnp.float32
    )


def kernel(
    rhs_hbm, diag_ref, coup_ref, carry_hbm, arrow_hbm, tip_right_hbm, tip_inverse_hbm,
    out_ref, tip_ref,
    rhs_ref, carry_ref, arrow_ref, tip_right_ref, tip_inverse_ref,
    mats, gathered, arriving, part_a, part_b, send_a, send_b, recv_a, recv_b,
    state_a, state_b, flipped, relay, relay_carry, arrow_line, turned, leaving, line_sum, line_heard, plane_sum, plane_heard,
    load_sem, mat_send, mat_recv, mat_local, sib_send, sib_recv,
    relay_recv, relay_send, carry_recv, carry_send,
    turn_send, turn_recv, vec_send, vec_recv,
    a_send, a_recv, b_send, b_recv, next_send, next_recv,
    arrow_sib_send, arrow_sib_recv, arrow_send, arrow_recv, arrow_local,
    out_send, out_recv, line_send, line_recv, plane_send, plane_recv,
):
    x = lax.axis_index("tm")
    place = lax.axis_index("mesh")
    y, z, core = place // (2 * SIDE), lax.rem(place // 2, SIDE), lax.rem(place, 2)
    other = 1 - core
    shard = rhs_ref.shape[1]
    chip = 2 * shard
    span = SIDE * chip
    lane = rhs_ref.shape[2] // 2
    chunks = lane // CHUNK
    effects = tip_ref.shape[0]
    sibling = device(x, y, z, other)
    along_z = lambda r: device(x, y, z + r, core)
    along_y = lambda r: device(x, y + r, z, core)
    along_x = lambda r: device(x + r, y, z, core)
    across_x = lambda r: device(x + r, y, z, other)
    steps = range(1, SIDE)

    loads = [
        pltpu.make_async_copy(src, dst, load_sem.at[i])
        for i, (src, dst) in enumerate((
            (rhs_hbm, rhs_ref), (carry_hbm, carry_ref), (arrow_hbm, arrow_ref),
            (tip_right_hbm, tip_right_ref), (tip_inverse_hbm, tip_inverse_ref),
        ))
    ]
    for load in loads:
        load.start()


    def aligned(value, unit):
        return pl.multiple_of(value, unit)

    def remote(src, dst, send, recv, target):
        return pltpu.make_async_remote_copy(
            src_ref=src, dst_ref=dst, send_sem=send, recv_sem=recv,
            device_id=target, device_id_type=MESH,
        )

    barrier = pltpu.get_barrier_semaphore()
    neighbours = [f(r) for f in (along_z, along_y, along_x, across_x) for r in steps]
    neighbours += [sibling]
    neighbours += [device(x + d, y + a, z + b, core) for d in (1, 3) for a, b in ((0, 2), (2, 0))]
    for target in neighbours:
        pl.semaphore_signal(barrier, inc=1, device_id=target, device_id_type=MESH)

    targets = (gathered.at[0], relay_carry, gathered.at[1])
    vec_lines = (along_y, along_y, along_z)
    vec_mine = (y, y, z)

    def slot(v, at, half):
        return targets[v].at[:, pl.ds(aligned(at * chip + half * shard, shard), shard)]

    def turn(v, value):
        value = value.T
        mine, theirs = value[:lane], value[lane:]
        mine, theirs = jnp.where(core == 0, mine, theirs), jnp.where(core == 0, theirs, mine)
        slot(v, vec_mine[v], core)[...] = mine
        turned[v] = theirs

    loads[0].wait()
    loads[1].wait()
    turn(0, rhs_ref[0])
    pl.when(x == 1)(lambda: turn(1, carry_ref[...]))
    turn(2, rhs_ref[1])
    pl.semaphore_wait(barrier, len(neighbours))

    sources = (diag_ref.at[0], coup_ref.at[0], diag_ref.at[1], coup_ref.at[1])
    lines = (along_z, along_z, along_y, along_y)
    mine = (z, z, y, y)

    def pieces(m, r):
        target_at = lax.rem(mine[m] + r, SIDE)
        rows = pl.ds(aligned(mine[m] * chip + core * shard, shard), shard)
        if m < 2:
            return [
                (
                    sources[m].at[:, pl.ds(aligned(a * span + target_at * chip, chip), chip)],
                    mats.at[m, rows, pl.ds(a * chip, chip)],
                )
                for a in range(SIDE)
            ]
        return [
            (
                sources[m].at[:, pl.ds(aligned(target_at * span, span), span)],
                mats.at[m, rows, :],
            )
        ]

    def send_near(m):
        for r in (1, 3):
            for src, dst in pieces(m, r):
                remote(src, dst, mat_send.at[m, r], mat_recv.at[m, r], lines[m](r)).start()

    def send_far(m):
        for src, dst in pieces(m, 2):
            remote(src, dst, mat_send.at[m, 2], mat_recv.at[m, 2], lines[m](2)).start()

    def send_round(m):
        rows = shard - (96, 80)[m // 2]
        found = pieces(m, 2)
        width = span // len(found)
        for n, (src, dst) in enumerate(found):
            columns = pl.ds(n * width, width)
            target = device(x + 3, y, z + 2, core) if m < 2 else device(x + 3, y + 2, z, core)
            remote(
                src.at[pl.ds(rows, shard - rows)], relay.at[m, pl.ds(0, shard - rows), columns],
                mat_send.at[m, 2], relay_recv.at[m], target,
            ).start()
        start = aligned(mine[m] * chip + core * shard, shard)
        for n, (src, dst) in enumerate(found):
            columns = pl.ds(n * width, width)
            remote(
                src.at[pl.ds(0, rows)], mats.at[m, pl.ds(start, rows), columns],
                mat_send.at[m, 2], mat_recv.at[m, 2], lines[m](2),
            ).start()

    def pass_on(m):
        rows = (96, 80)[m // 2]
        at = lax.rem(mine[m] + 2, SIDE) * chip + core * shard + shard - rows
        dst = mats.at[m, pl.ds(aligned(at, 16), rows), :]
        return remote(
            relay.at[m, pl.ds(0, rows)], dst, relay_send.at[m], mat_recv.at[m, 2], device(0, y, z, core)
        )

    def relay_wait(m):
        held = relay.at[m, pl.ds(0, (96, 80)[m // 2])]
        remote(held, held, relay_send.at[m], relay_recv.at[m], device(0, y, z, core)).wait_recv()

    def send_local(m):
        for src, dst in pieces(m, 0):
            remote(src, dst, sib_send.at[m, 0], sib_recv.at[m, 0], sibling).start()
            pltpu.make_async_copy(src, dst, mat_local.at[m]).start()

    def block(m, r, half):
        at = lax.rem(mine[m] - r + SIDE, SIDE)
        return mats.at[m, pl.ds(aligned(at * chip + half * shard, shard), shard), :]

    def line_copy(m, r):
        rows = block(m, r, core)
        return remote(rows, rows, mat_send.at[m, r], mat_recv.at[m, r], lines[m](r))

    def sibling_copy(m, r, half):
        rows = block(m, r, half)
        return remote(rows, rows, sib_send.at[m, r], sib_recv.at[m, r], sibling)

    def flip(m, r, half):
        if m % 2:
            at = lax.rem(mine[m] - r + SIDE, SIDE)
            columns = pl.ds(aligned(at * chip + half * shard, shard), shard)
            flipped[m // 2, :, columns] = block(m, r, half)[...].T

    def forward(m):
        for r in (1, 3, 2):
            line_copy(m, r).wait_recv()
            sibling_copy(m, r, core).start()
            flip(m, r, core)

    def complete(m):
        rows = block(m, 0, core)
        pltpu.make_async_copy(rows, rows, mat_local.at[m]).wait()
        flip(m, 0, core)
        for r in (0, 1, 3, 2):
            sibling_copy(m, r, other).wait_recv()
            flip(m, r, other)

    def turn_copy(v):
        return remote(
            turned.at[v], slot(v, vec_mine[v], core), turn_send.at[v], turn_recv.at[v], sibling
        )

    def vec_copy(v, r, half):
        rows = slot(v, vec_mine[v], half)
        return remote(
            rows, rows, vec_send.at[v, r, half], vec_recv.at[v, r, half], vec_lines[v](r)
        )

    def vec_begin(v):
        turn_copy(v).start()
        for r in (2, 1, 3):
            vec_copy(v, r, core).start()

    def vec_rest(v):
        rows = slot(v, vec_mine[v], other)
        remote(rows, rows, turn_send.at[v], turn_recv.at[v], sibling).wait_recv()
        for r in (2, 1, 3):
            vec_copy(v, r, other).start()

    def vec_wait(v):
        for r in (1, 3, 2):
            for half in range(2):
                rows = slot(v, lax.rem(vec_mine[v] - r + SIDE, SIDE), half)
                remote(
                    rows, rows, vec_send.at[v, r, half], vec_recv.at[v, r, half], vec_lines[v](r)
                ).wait_recv()

    arrow_lines = (along_z, along_y)
    arrow_mine = (z, y)

    def arrow_slot(b, at, half):
        return arrow_line.at[b, :, pl.ds(aligned(at * chip + half * shard, shard), shard)]

    def arrow_local_copy(b):
        return pltpu.make_async_copy(
            arrow_ref.at[b], arrow_slot(b, arrow_mine[b], core), arrow_local.at[b]
        )

    def arrow_sibling_copy(b, half):
        return remote(
            arrow_ref.at[b], arrow_slot(b, arrow_mine[b], half),
            arrow_sib_send.at[b], arrow_sib_recv.at[b], sibling,
        )

    def arrow_copy(b, r, at):
        rows = arrow_line.at[b, :, pl.ds(aligned(at * chip, chip), chip)]
        return remote(rows, rows, arrow_send.at[b, r], arrow_recv.at[b, r], arrow_lines[b](r))

    def carry_copy():
        return remote(relay_carry, arriving, carry_send, carry_recv, device(0, y, z, core))

    pl.when(x == 1)(lambda: vec_begin(1))
    vec_begin(0)

    @pl.when(x == 0)
    def _():
        for m in range(2):
            send_round(m)

    @pl.when(x < 3)
    def _():
        for m in range(2):
            send_near(m)

    turn_copy(2).start()
    pl.when(x == 1)(lambda: vec_rest(1))
    vec_rest(0)

    @pl.when(x == 0)
    def _():
        for m in range(2, 4):
            send_round(m)

    @pl.when(x < 3)
    def _():
        for m in range(2, 4):
            send_near(m)

    @pl.when(jnp.logical_or(x == 1, x == 2))
    def _():
        for m in range(4):
            send_far(m)

    for m in range(4):
        send_local(m)

    @pl.when(x == 1)
    def _():
        vec_wait(1)
        carry_copy().start()

    @pl.when(x == 3)
    def _():
        for m in (0, 1):
            relay_wait(m)
            pass_on(m).start()
        for m in (2, 3):
            relay_wait(m)
            pass_on(m).start()
        for m in range(4):
            send_near(m)
        for m in range(4):
            send_far(m)

    loads[2].wait()
    for b in range(2):
        arrow_local_copy(b).start()
        arrow_sibling_copy(b, core).start()

    forward(0)
    for r in (2, 1, 3):
        vec_copy(2, r, core).start()
    vec_rest(2)
    vec_wait(0)
    complete(0)
    part_a[...] = times_transposed(gathered[0], mats[0])
    forward(1)
    complete(1)

    @pl.when(x == 0)
    def _():
        carry_copy().wait_recv()

    def rows_of(k):
        return pl.ds(aligned(k * CHUNK, CHUNK), CHUNK)

    def chunk_copy(src, dst, send, recv, line, k, r, columns=slice(None)):
        return remote(
            src.at[rows_of(k), columns], dst.at[r - 1, rows_of(k), columns],
            send.at[k, r], recv.at[k, r], line(r),
        )

    copy_a = functools.partial(chunk_copy, send_a, recv_a, a_send, a_recv, along_z)
    copy_b = functools.partial(chunk_copy, send_b, recv_b, b_send, b_recv, along_y)

    def copy_next(k):
        return remote(
            state_b.at[rows_of(k)], arriving.at[rows_of(k)], next_send.at[k], next_recv.at[k], along_x(1)
        )

    def spread(terms, sent, matrix, source, copy, k):
        rows = rows_of(k)
        width = span // 2
        for h in range(2):
            columns = pl.ds(h * width, width)
            value = terms[rows, columns] - jnp.dot(
                source[rows, :], matrix[:, columns], preferred_element_type=jnp.float32
            )
            terms[rows, columns] = value
            sent[rows, columns] = value.astype(jnp.bfloat16)
            for r in (2, 1, 3):
                copy(k, r, columns).start()

    def settle(terms, received, state, copy, k):
        rows = rows_of(k)
        for r in (1, 3, 2):
            copy(k, r).wait_recv()
        value = terms[rows, :]
        for r in steps:
            value = value + received[r - 1, rows, :].astype(jnp.float32)
        state[rows, :] = value.astype(jnp.bfloat16)

    def first(k):
        @pl.when(x > 0)
        def _():
            copy_next(k).wait_recv()

        spread(part_a, send_a, flipped.at[0], arriving, copy_a, k)

    def second(k):
        settle(part_a, recv_a, state_a, copy_a, k)
        spread(part_b, send_b, flipped.at[1], state_a, copy_b, k)

    def third(k):
        settle(part_b, recv_b, state_b, copy_b, k)

        @pl.when(x < SIDE - 1)
        def _():
            copy_next(k).start()

    def second_block():
        forward(2)
        forward(3)
        vec_wait(2)
        complete(2)
        part_b[...] = times_transposed(gathered[1], mats[2])
        complete(3)
        for b in range(2):
            arrow_sibling_copy(b, other).wait_recv()
            arrow_local_copy(b).wait()
            for r in steps:
                arrow_copy(b, r, arrow_mine[b]).start()

    pl.when(x > 0)(second_block)

    def lead(k, carry):
        first(k)
        return carry

    lax.fori_loop(0, AHEAD, lead, 0)
    pl.when(x == 0)(second_block)

    def step(n, carry):
        @pl.when(n >= 2 * AHEAD)
        def _():
            third(n - 2 * AHEAD)

        @pl.when(jnp.logical_and(n >= AHEAD, n < chunks + AHEAD))
        def _():
            second(n - AHEAD)

        @pl.when(n < chunks)
        def _():
            first(n)

        return carry

    sum_lines = (along_y, along_z)
    half_lane = lane // 2

    def line_copy_of(b, h, r):
        return remote(
            line_sum.at[b, h], line_heard.at[b, h, r - 1],
            line_send.at[b, h, r], line_recv.at[b, h, r], sum_lines[b](r),
        )

    def line_begin(b, h):
        state = (state_a, state_b)[b]
        line_sum[b, h] = times_transposed(
            arrow_line[b], state[pl.ds(h * half_lane, half_lane), :]
        )
        for r in (2, 1, 3):
            line_copy_of(b, h, r).start()

    def plane_targets(h):
        found = []
        for r in range(SIDE):
            if r:
                found.append((0, r, along_x(r)))
            found.append((1, r, across_x(r) if r else sibling))
        return [
            remote(
                plane_sum.at[h], plane_heard.at[h, cross, r],
                plane_send.at[h, cross, r], plane_recv.at[h, cross, r], target,
            )
            for cross, r, target in found
        ]

    def plane_begin(h):
        value = jnp.zeros((effects, half_lane), jnp.float32)
        for b in range(2):
            value = value + line_sum[b, h]
            for r in steps:
                line_copy_of(b, h, r).wait_recv()
                value = value + line_heard[b, h, r - 1]
        plane_sum[h] = value
        for copy in plane_targets(h):
            copy.start()

    middle = chunks // 2 + 2 * AHEAD
    lax.fori_loop(AHEAD, middle, step, 0)
    for b in range(2):
        for r in steps:
            arrow_copy(b, r, lax.rem(arrow_mine[b] - r + SIDE, SIDE)).wait_recv()
    line_begin(0, 0)
    line_begin(1, 0)
    lax.fori_loop(middle, chunks + 2 * AHEAD, step, 0)
    line_begin(1, 1)
    line_begin(0, 1)
    plane_begin(0)

    def out_copy(b, columns):
        return remote(
            leaving.at[b], out_ref.at[b, :, columns], out_send.at[b], out_recv.at[b], sibling
        )

    own_columns = pl.ds(aligned(core * lane, lane), lane)
    other_columns = pl.ds(aligned(other * lane, lane), lane)
    for b, (state, at) in enumerate([(state_a, z), (state_b, y)]):
        start = at * chip
        leaving[b] = state[:, pl.ds(aligned(start + other * shard, shard), shard)].T
        out_copy(b, own_columns).start()
        out_ref[b, :, own_columns] = state[:, pl.ds(aligned(start + core * shard, shard), shard)].T

    plane_begin(1)

    for m in range(4):
        for r in steps:
            line_copy(m, r).wait_send()
        for r in range(SIDE):
            sibling_copy(m, r, core).wait_send()

    def vec_drain(v):
        turn_copy(v).wait_send()
        for r in steps:
            for half in range(2):
                vec_copy(v, r, half).wait_send()

    vec_drain(0)

    @pl.when(x == 1)
    def _():
        vec_drain(1)
        carry_copy().wait_send()

    @pl.when(x == 3)
    def _():
        for m in range(4):
            pass_on(m).wait_send()

    vec_drain(2)
    for b in range(2):
        arrow_sibling_copy(b, core).wait_send()
        for r in steps:
            arrow_copy(b, r, arrow_mine[b]).wait_send()

    def drain(k, carry):
        for r in steps:
            copy_a(k, r).wait_send()
            copy_b(k, r).wait_send()

        @pl.when(x < SIDE - 1)
        def _():
            copy_next(k).wait_send()

        return carry

    lax.fori_loop(0, chunks, drain, 0)
    for b in range(2):
        out_copy(b, own_columns).wait_send()
        out_copy(b, other_columns).wait_recv()
        for h in range(2):
            for r in steps:
                line_copy_of(b, h, r).wait_send()
    loads[3].wait()
    loads[4].wait()

    for h in range(2):
        for copy in plane_targets(h):
            copy.wait_send()
            copy.wait_recv()
        for cross, owner in enumerate((core, other)):
            value = plane_heard[h, 1, 0] if cross else plane_sum[h]
            for r in steps:
                value = value + plane_heard[h, cross, r]
            columns = pl.ds(aligned(owner * lane + h * half_lane, half_lane), half_lane)
            tip_ref[:, columns] = jnp.dot(
                tip_inverse_ref[...],
                tip_right_ref[:, columns] - value,
                precision=lax.Precision.HIGHEST,
                preferred_element_type=jnp.float32,
            )


def body(right_sides, diag_inverse, coupling, carry_in, arrow_blocks, tip_right, tip_inverse):
    blocks, shard, columns = right_sides.shape
    effects = tip_right.shape[0]
    chip, span, lane = 2 * shard, 2 * shard * SIDE, columns // 2
    chunks = lane // CHUNK
    vmem = pl.BlockSpec(memory_space=pltpu.VMEM)
    hbm = pl.BlockSpec(memory_space=pl.ANY)
    half, full = jnp.bfloat16, jnp.float32
    dma = pltpu.SemaphoreType.DMA
    return pl.pallas_call(
        kernel,
        out_shape=(
            jax.ShapeDtypeStruct(right_sides.shape, half),
            jax.ShapeDtypeStruct(tip_right.shape, full),
        ),
        in_specs=[hbm] * 7,
        out_specs=(vmem, vmem),
        scratch_shapes=[
            pltpu.VMEM(right_sides.shape, half),
            pltpu.VMEM(carry_in.shape, half),
            pltpu.VMEM(arrow_blocks.shape, half),
            pltpu.VMEM(tip_right.shape, full),
            pltpu.VMEM(tip_inverse.shape, full),
            pltpu.VMEM((4, span, span), half),
            pltpu.VMEM((2, lane, span), half),
            pltpu.VMEM((lane, span), half),
            pltpu.VMEM((lane, span), full),
            pltpu.VMEM((lane, span), full),
            pltpu.VMEM((lane, span), half),
            pltpu.VMEM((lane, span), half),
            pltpu.VMEM((SIDE - 1, lane, span), half),
            pltpu.VMEM((SIDE - 1, lane, span), half),
            pltpu.VMEM((lane, span), half),
            pltpu.VMEM((lane, span), half),
            pltpu.VMEM((2, span, span), half),
            pltpu.VMEM((4, shard, span), half),
            pltpu.VMEM((lane, span), half),
            pltpu.VMEM((blocks, effects, span), half),
            pltpu.VMEM((3, lane, shard), half),
            pltpu.VMEM((blocks, shard, lane), half),
            pltpu.VMEM((2, 2, effects, lane // 2), full),
            pltpu.VMEM((2, 2, SIDE - 1, effects, lane // 2), full),
            pltpu.VMEM((2, effects, lane // 2), full),
            pltpu.VMEM((2, 2, SIDE, effects, lane // 2), full),
            dma((5,)), dma((4, SIDE)), dma((4, SIDE)), dma((4,)), dma((4, SIDE)), dma((4, SIDE)),
            dma((4,)), dma((4,)), dma, dma,
            dma((3,)), dma((3,)), dma((3, SIDE, 2)), dma((3, SIDE, 2)),
            dma((chunks, SIDE)), dma((chunks, SIDE)), dma((chunks, SIDE)), dma((chunks, SIDE)),
            dma((chunks,)), dma((chunks,)),
            dma((2,)), dma((2,)), dma((2, SIDE)), dma((2, SIDE)), dma((2,)),
            dma((2,)), dma((2,)), dma((2, 2, SIDE)), dma((2, 2, SIDE)), dma((2, 2, SIDE)), dma((2, 2, SIDE)),
        ],
        compiler_params=pltpu.CompilerParams(
            collective_id=0, has_side_effects=True, vmem_limit_bytes=VMEM_LIMIT
        ),
    )(right_sides, diag_inverse, coupling, carry_in, arrow_blocks, tip_right, tip_inverse)


def solution(mesh):
    placed = (
        P("tm", "mesh", None),
        P("tm", "mesh", None),
        P("tm", "mesh", None),
        P("mesh", None),
        P("tm", None, "mesh"),
        P(),
        P(),
    )
    return jax.shard_map(
        body, mesh=mesh, in_specs=placed, out_specs=(P("tm", "mesh", None), P()), check_vma=False
    )
```
